512 devices in a mesh: grid: 64 (over x_lo, z, core), dp: 8 (over y, x_hi).
Axes of the slice: x: 4 (x_hi: 2, x_lo: 2; x = x_hi * 2 + x_lo), y: 4, z: 16, core: 2. Of those that a mesh axis runs over, the one named last changes fastest.
Arguments:
- in_field: bfloat16 [8, 512, 64, 512], P('dp', 'grid'), may hold values from -6 to 6
- out_grad: bfloat16 [8, 512, 64, 512], P('dp', 'grid'), may hold values from -6 to 6
- point_weight: bfloat16 [64, 64], replicated, may hold values from -0.75 to 0.75
- point_bias: float32 [64], replicated, may hold values from -3 to 3
- spectral_weight: float32 [64, 64, 2, 4096], P('dp', 'grid'), may hold values from -3 to 3
- first_moment: float32 [64, 64, 2, 4096], P('dp', 'grid'), may hold values from -8 to 8
- second_moment: float32 [64, 64, 2, 4096], P('dp', 'grid'), may hold values from 1 to 40
Outputs:
- grad_field: bfloat16 [8, 512, 64, 512], P('dp', 'grid')
- new_weight: float32 [64, 64, 2, 4096], P('dp', 'grid')
- new_first: float32 [64, 64, 2, 4096], P('dp', 'grid')
- new_second: float32 [64, 64, 2, 4096], P('dp', 'grid')
The draws below stay inside these ranges and needn't reach their ends.
All inputs are finite; a program needn't handle non-finite values.
Results may differ from the reference program's by a relative error of at most 0.019.
Values may be sent and summed in bfloat16 or wider, within the bound.
No kernel may reach another device: no remote copies, remote signals or barrier semaphores. Data moves between devices by JAX's collectives and lax.ppermute only.
A program may use at most 128 MiB of HBM per device.

```python
import math
import jax
import jax.numpy as jnp
from jax import lax

C = 64
NX = 512
NY = 512
MX = 64
MY = 64
SAMPLES = 8


def block_scale(key, extent, cuts, smallest, high):
    def one(axis_at, shards_of):
        heights = jax.random.uniform(jax.random.fold_in(jax.random.fold_in(key, 6), axis_at), (shards_of,), jnp.float32, smallest / len(cuts), high / len(cuts))
        return jnp.repeat(jnp.exp(heights), extent[axis_at] // shards_of).reshape((-1,) + (1,) * (len(extent) - axis_at - 1))

    factor_of = one(*cuts[0])
    for cut in cuts[1:]:
        factor_of = factor_of * one(*cut)
    return factor_of


def scatter_about(key, shape, scale, most, shards=(), held_as=jnp.bfloat16):
    gain = block_scale(key, shape, shards, -0.22, 0.18) if shards else 1.0
    drawn = jax.random.normal(key, shape, jnp.float32) * scale * gain
    return jnp.minimum(jnp.maximum(drawn, -most), most).astype(held_as)


def setup_inputs(seed: int = 0) -> dict:
    seeds = jax.random.split(jax.random.key(seed), 8)
    return {
        "in_field": scatter_about(seeds[0], (SAMPLES, NX, C, NY), 1.0, 6.0, ((0, 8), (1, 64))),
        "out_grad": scatter_about(seeds[1], (SAMPLES, NX, C, NY), 1.0, 6.0, ((0, 8), (1, 64))),
        "point_weight": scatter_about(seeds[2], (C, C), C ** -0.5, 0.75),
        "point_bias": scatter_about(seeds[3], (C,), 0.5, 3.0, (), jnp.float32),
        "spectral_weight": scatter_about(seeds[4], (MX, MY, 2, C * C), 0.5, 3.0, ((0, 8), (1, 64)), jnp.float32),
        "first_moment": scatter_about(seeds[5], (MX, MY, 2, C * C), 2.0, 8.0, ((0, 8), (1, 64)), jnp.float32),
        "second_moment": jnp.clip(jnp.exp(math.log(40.0) - 3.6888795 * jax.random.uniform(seeds[6], (MX, MY, 2, C * C), jnp.float32) ** block_scale(seeds[6], (MX, MY, 2, C * C), ((0, 8), (1, 64)), -0.2, 0.2)), 1.0, 40.0),
    }


beta_one = 0.9
beta_two = 0.999
learn_rate = 0.01
adam_step = 100
epsilon_adam = 1e-08

def widened(array):
    return array.astype(jnp.float32)

def row_tables():
    frequency = jnp.arange(MY, dtype=jnp.int32)
    position = jnp.arange(NY, dtype=jnp.int32)
    angles = (position[:, None] * frequency[None, :] % NY).astype(jnp.float32) * (2.0 * math.pi / NY)
    forward = jnp.stack([jnp.cos(angles), -jnp.sin(angles)], axis=-1).reshape(NY, 2 * MY).astype(jnp.bfloat16)
    factor = jnp.where(frequency == 0, 1.0, 2.0).astype(jnp.float32) / (NX * NY)
    inverse = jnp.stack([factor * jnp.cos(angles), -factor * jnp.sin(angles)], axis=-1)
    inverse = inverse.reshape(NY, 2 * MY).T.astype(jnp.bfloat16)
    return (forward, inverse)

def column_tables():
    column = jnp.arange(MX, dtype=jnp.int32)
    wavenumber = jnp.where(column < MX // 2, column, NX - MX + column)
    position = jnp.arange(NX, dtype=jnp.int32)
    angles = (wavenumber[:, None] * position[None, :] % NX).astype(jnp.float32) * (2.0 * math.pi / NX)
    return (jnp.cos(angles).astype(jnp.bfloat16), jnp.sin(angles).astype(jnp.bfloat16))

def gelu_slope(value):
    return 0.5 * (1.0 + lax.erf(value / math.sqrt(2.0))) + value * jnp.exp(-0.5 * value * value) / math.sqrt(2.0 * math.pi)

def reference(in_field, out_grad, point_weight, point_bias, spectral_weight, first_moment, second_moment):
    row_forward, row_inverse = row_tables()
    col_cos, col_sin = column_tables()
    forward_wide, inverse_wide = (widened(row_forward), widened(row_inverse))
    cos_wide, sin_wide = (widened(col_cos), widened(col_sin))
    mixing = spectral_weight.astype(jnp.bfloat16).reshape(MX, MY, 2, C, C)
    mix_real, mix_imaginary = (widened(mixing[:, :, 0]), widened(mixing[:, :, 1]))
    point_wide = widened(point_weight)

    def to_modes(spectra):
        wide = widened(spectra).reshape(NX, C, MY, 2)
        real_part, imaginary_part = (wide[..., 0], wide[..., 1])
        out_real = jnp.einsum('kx,xcq->kcq', cos_wide, real_part) + jnp.einsum('kx,xcq->kcq', sin_wide, imaginary_part)
        out_imaginary = jnp.einsum('kx,xcq->kcq', cos_wide, imaginary_part) - jnp.einsum('kx,xcq->kcq', sin_wide, real_part)
        return (out_real.astype(jnp.bfloat16), out_imaginary.astype(jnp.bfloat16))

    def to_rows(modes_real, modes_imaginary):
        real_part, imaginary_part = (widened(modes_real), widened(modes_imaginary))
        row_real = jnp.einsum('kx,kcq->xcq', cos_wide, real_part) - jnp.einsum('kx,kcq->xcq', sin_wide, imaginary_part)
        row_imaginary = jnp.einsum('kx,kcq->xcq', sin_wide, real_part) + jnp.einsum('kx,kcq->xcq', cos_wide, imaginary_part)
        return jnp.stack([row_real, row_imaginary], axis=-1).reshape(NX, C, 2 * MY).astype(jnp.bfloat16)

    def per_sample(pair):
        sample, cotangent = pair
        wide_field = widened(sample)
        spectra = jnp.einsum('xcy,yj->xcj', wide_field, forward_wide).astype(jnp.bfloat16)
        field_real, field_imaginary = to_modes(spectra)
        wide_real, wide_imaginary = (widened(field_real), widened(field_imaginary))
        mixed_real = jnp.einsum('kcq,kqco->koq', wide_real, mix_real) - jnp.einsum('kcq,kqco->koq', wide_imaginary, mix_imaginary)
        mixed_imaginary = jnp.einsum('kcq,kqco->koq', wide_real, mix_imaginary) + jnp.einsum('kcq,kqco->koq', wide_imaginary, mix_real)
        mixed_rows = to_rows(mixed_real.astype(jnp.bfloat16), mixed_imaginary.astype(jnp.bfloat16))
        spectral_out = jnp.einsum('xcj,jy->xcy', widened(mixed_rows), inverse_wide)
        linear = jnp.einsum('xcy,co->xoy', wide_field, point_wide)
        pre_activation = spectral_out + linear + point_bias[None, :, None]
        pre_grad = (widened(cotangent) * gelu_slope(pre_activation)).astype(jnp.bfloat16)
        wide_grad = widened(pre_grad)
        back_spectra = jnp.einsum('xoy,jy->xoj', wide_grad, inverse_wide).astype(jnp.bfloat16)
        back_real, back_imaginary = to_modes(back_spectra)
        grad_real, grad_imaginary = (widened(back_real), widened(back_imaginary))
        input_real = jnp.einsum('koq,kqco->kcq', grad_real, mix_real) + jnp.einsum('koq,kqco->kcq', grad_imaginary, mix_imaginary)
        input_imaginary = jnp.einsum('koq,kqco->kcq', grad_imaginary, mix_real) - jnp.einsum('koq,kqco->kcq', grad_real, mix_imaginary)
        input_rows = to_rows(input_real.astype(jnp.bfloat16), input_imaginary.astype(jnp.bfloat16))
        input_grad = jnp.einsum('xoy,co->xcy', wide_grad, point_wide) + jnp.einsum('xcj,yj->xcy', widened(input_rows), forward_wide)
        return (input_grad.astype(jnp.bfloat16), field_real, field_imaginary, back_real, back_imaginary)
    grad_field, field_real, field_imaginary, back_real, back_imaginary = lax.map(per_sample, (in_field, out_grad))
    wide_sr, wide_si = (widened(field_real), widened(field_imaginary))
    wide_gr, wide_gi = (widened(back_real), widened(back_imaginary))
    weight_real = jnp.einsum('bkcq,bkoq->kqco', wide_sr, wide_gr) + jnp.einsum('bkcq,bkoq->kqco', wide_si, wide_gi)
    weight_imaginary = jnp.einsum('bkcq,bkoq->kqco', wide_sr, wide_gi) - jnp.einsum('bkcq,bkoq->kqco', wide_si, wide_gr)
    gradient = jnp.stack([weight_real, weight_imaginary], axis=2).reshape(MX, MY, 2, C * C)
    new_first = beta_one * first_moment + (1.0 - beta_one) * gradient
    new_second = beta_two * second_moment + (1.0 - beta_two) * gradient * gradient
    bias_one = 1.0 - beta_one ** adam_step
    bias_two = 1.0 - beta_two ** adam_step
    update = learn_rate * (new_first / bias_one) / (jnp.sqrt(new_second / bias_two) + epsilon_adam)
    new_weight = spectral_weight - update
    return (grad_field, new_weight, new_first, new_second)
```

```python
import math

import jax
import jax.numpy as jnp
import numpy as np
from jax import lax
from jax.experimental import pallas as pl
from jax.experimental.pallas import tpu as pltpu
from jax.sharding import PartitionSpec as P

C = 64
NX = 512
NY = 512
MX = 64
MY = 64
SLAB = 8
QUAD = 4
HALF = 64
BLOCKS = 8

beta_one = 0.9
beta_two = 0.999
learn_rate = 0.01
adam_step = 100
epsilon_adam = 1e-08

f32 = jnp.float32
bf16 = jnp.bfloat16


def tables():
    frequency = np.arange(MY)
    position = np.arange(NY)
    angles = ((position[:, None] * frequency[None, :]) % NY).astype(np.float32) * np.float32(
        2.0 * math.pi / NY
    )
    cos, sin = np.cos(angles), np.sin(angles)
    forward = np.stack([cos, -sin], axis=-1).reshape(NY, 2 * MY).T
    factor = np.where(frequency == 0, 1.0, 2.0).astype(np.float32) / np.float32(NX * NY)
    inverse = np.stack([factor * cos, -factor * sin], axis=-1).reshape(NY, 2 * MY).T

    column = np.arange(MX)
    wavenumber = np.where(column < MX // 2, column, NX - MX + column)
    rows = np.arange(NX)
    turn = ((wavenumber[:, None] * rows[None, :]) % NX).astype(np.float32) * np.float32(
        2.0 * math.pi / NX
    )
    col_cos, col_sin = np.cos(turn), np.sin(turn)

    by_slab = lambda t: t.reshape(BLOCKS, 8, NX // SLAB, QUAD, 2)
    c, s = by_slab(col_cos), by_slab(col_sin)
    to_modes = np.stack([np.stack([c, s], 0), np.stack([-s, c], 0)], 0)
    to_modes = to_modes.transpose(6, 2, 0, 3, 4, 1, 5).reshape(256, 512)

    by_slab = lambda t: t.reshape(MX, NX // SLAB, QUAD, 2)
    c, s = by_slab(col_cos), by_slab(col_sin)
    to_rows = np.stack([np.stack([c, -s], 0), np.stack([s, c], 0)], 0)
    to_rows = to_rows.transpose(3, 0, 4, 1, 5, 2).reshape(512, 256)

    weave = np.eye(512, dtype=np.float32).reshape(QUAD, 128, 512).transpose(1, 0, 2).reshape(512, 512)

    pick = np.zeros((4, 8, 8, 2, 8, 2, 8), np.float32)
    for b in range(8):
        for j in range(8):
            for p in range(2):
                pick[0, b, j, p, b, 0, j] = 1.0
                pick[1, b, j, p, b, 1, j] = 1.0
                pick[2, b, j, p, b, p, j] = 1.0
                pick[3, b, j, p, b, 1 - p, j] = 1.0 - 2.0 * p
    pick = pick.reshape(512, 128)
    made = (forward, inverse, to_modes, to_rows, weave, pick)
    return tuple(np.asarray(t, np.float32).astype(jnp.bfloat16) for t in made)


def mm(a, b):
    return lax.dot_general(a, b, (((1,), (0,)), ((), ())), preferred_element_type=f32)


def mm_nt(a, b):
    return lax.dot_general(a, b, (((1,), (1,)), ((), ())), preferred_element_type=f32)


def mm_tn(a, b):
    return lax.dot_general(a, b, (((0,), (0,)), ((), ())), preferred_element_type=f32)


def low_lanes(shape):
    return lax.broadcasted_iota(jnp.int32, shape, len(shape) - 1) % 128 < HALF


def swap(value):
    return jnp.concatenate([value[:, HALF:], value[:, :HALF]], axis=1)


def spectra_of(table, rows):
    return mm_nt(table, rows).astype(bf16)


def modes_of(received, to_modes):
    both = mm(to_modes, received)
    chosen = jnp.where(low_lanes((128, 128)), both[:128], both[128:])
    return (chosen + swap(chosen)).astype(bf16)


def rows_of(modes, to_rows):
    low = low_lanes((MX, 128))
    turned = swap(modes)
    stacked = jnp.concatenate(
        [
            jnp.where(low, modes, 0.0),
            jnp.where(low, 0.0, turned),
            jnp.where(low, turned, 0.0),
            jnp.where(low, 0.0, modes),
        ],
        axis=0,
    ).astype(bf16)
    return mm(to_rows, stacked).astype(bf16)


def own_block(shape):
    return (
        lax.broadcasted_iota(jnp.int32, shape, 0) % 8
        == lax.broadcasted_iota(jnp.int32, shape, 1) // HALF
    )


def gelu_slope(value):
    return 0.5 * (1.0 + lax.erf(value / math.sqrt(2.0))) + value * jnp.exp(
        -0.5 * value * value
    ) / math.sqrt(2.0 * math.pi)


def spectra_kernel(field_ref, table_ref, weave_ref, out_ref):
    table = table_ref[...]
    parts = [
        spectra_of(table, field_ref[q * 128 : (q + 1) * 128, :]) for q in range(QUAD)
    ]
    out_ref[...] = mm(weave_ref[...], jnp.concatenate(parts, axis=0)).astype(bf16)


def forward_modes_kernel(received_ref, weight_ref, to_modes_ref, to_rows_ref, modes_ref, out_ref):
    modes = modes_of(received_ref[...], to_modes_ref[...])
    modes_ref[...] = modes
    wide = modes.astype(f32)
    own = own_block((16, 512))
    sign = jnp.where(low_lanes((8, 128)), -1.0, 1.0)
    mixed = []
    for block in range(BLOCKS):
        mine = wide[block * 16 : (block + 1) * 16]
        spread = jnp.where(own, jnp.concatenate([mine] * 4, axis=1), 0.0).astype(bf16)
        product = mm(spread, weight_ref[block * 512 : (block + 1) * 512, :])
        mixed.append(product[:8] + sign * swap(product[8:]))
    out_ref[...] = rows_of(jnp.concatenate(mixed, axis=0), to_rows_ref[...])


def backward_modes_kernel(
    received_ref, weight_ref, modes_ref, to_modes_ref, to_rows_ref, pair_ref, out_ref
):
    grads = modes_of(received_ref[...], to_modes_ref[...])
    wide = grads.astype(f32)
    pair_ref[...] = jnp.where(
        low_lanes((128, 128)), modes_ref[...].astype(f32), wide
    ).astype(bf16)
    own = own_block((16, 512))
    low = low_lanes((8, 128))
    mixed = []
    for block in range(BLOCKS):
        real = wide[block * 16 : block * 16 + 8]
        imaginary = wide[block * 16 + 8 : block * 16 + 16]
        turned = jnp.concatenate(
            [jnp.where(low, real, imaginary), jnp.where(low, imaginary, -real)], axis=0
        ).astype(bf16)
        product = mm_nt(turned, weight_ref[block * 512 : (block + 1) * 512, :])
        product = jnp.where(own, product, 0.0)
        folded = product[:, :128] + product[:, 128:256] + product[:, 256:384] + product[:, 384:]
        folded = folded + swap(folded)
        mixed.append(jnp.where(low, folded[:8], folded[8:]))
    out_ref[...] = rows_of(jnp.concatenate(mixed, axis=0), to_rows_ref[...])


def slope_kernel(
    received_ref,
    field_ref,
    cotangent_ref,
    point_ref,
    bias_ref,
    inverse_ref,
    weave_ref,
    grad_ref,
    out_ref,
):
    inverse = inverse_ref[...]
    weave = weave_ref[...]
    rows = mm_tn(weave, received_ref[...]).astype(bf16)
    parts = []
    for q in range(QUAD):
        at = slice(q * 128, (q + 1) * 128)
        value = mm_tn(rows[at], inverse) + mm(point_ref[...], field_ref[at, :]) + bias_ref[...]
        grad = (cotangent_ref[at, :].astype(f32) * gelu_slope(value)).astype(bf16)
        grad_ref[at, :] = grad
        parts.append(spectra_of(inverse, grad))
    out_ref[...] = mm(weave, jnp.concatenate(parts, axis=0)).astype(bf16)


def field_kernel(received_ref, grad_ref, point_ref, forward_ref, weave_ref, out_ref):
    forward = forward_ref[...]
    rows = mm_tn(weave_ref[...], received_ref[...]).astype(bf16)
    for q in range(QUAD):
        at = slice(q * 128, (q + 1) * 128)
        value = mm_tn(rows[at], forward) + mm(point_ref[...], grad_ref[at, :])
        out_ref[at, :] = value.astype(bf16)


def adam_kernel(
    pair_ref, pick_ref, weight_ref, first_ref, second_ref, new_weight_ref, new_first_ref, new_second_ref
):
    width = 512
    bias_one = 1.0 - beta_one**adam_step
    bias_two = 1.0 - beta_two**adam_step
    picked = mm(pick_ref[...], pair_ref[...]).astype(bf16)
    row = lax.broadcasted_iota(jnp.int32, (128, width), 0)
    lane = lax.broadcasted_iota(jnp.int32, (128, width), 1)
    outer = jnp.where(row == HALF + lane % HALF, 1.0, 0.0).astype(bf16)
    right_one = mm(picked[256:384], outer)
    right_two = mm(picked[384:], outer)
    for n in range(C * C // width):
        inner = jnp.where(row == n * (width // HALF) + lane // HALF, 1.0, 0.0).astype(bf16)
        product = mm(picked[:128], inner) * right_one + mm(picked[128:256], inner) * right_two
        gradient = product[:16]
        for b in range(1, 8):
            gradient = gradient + product[b * 16 : (b + 1) * 16]
        at = slice(n * width, (n + 1) * width)
        first = beta_one * first_ref[:, at] + (1.0 - beta_one) * gradient
        second = beta_two * second_ref[:, at] + (1.0 - beta_two) * gradient * gradient
        new_first_ref[:, at] = first
        new_second_ref[:, at] = second
        step = learn_rate * (first / bias_one) / (jnp.sqrt(second / bias_two) + epsilon_adam)
        new_weight_ref[:, at] = weight_ref[:, at] - step


def call(kernel, outs, *arrays):
    return pl.pallas_call(
        kernel,
        out_shape=[jax.ShapeDtypeStruct(shape, dtype) for shape, dtype in outs],
        compiler_params=pltpu.CompilerParams(vmem_limit_bytes=40 * 1024 * 1024),
    )(*arrays)


def exchange(array, axis):
    return lax.all_to_all(array, axis, split_axis=0, concat_axis=0, tiled=True)


def shards(
    in_field, out_grad, point_weight, point_bias, spectral_weight, first_moment, second_moment
):
    forward, inverse, to_modes, to_rows, weave, pick = (jnp.asarray(t) for t in tables())
    field = in_field.reshape(SLAB * C, NY)
    cotangent = out_grad.reshape(SLAB * C, NY)
    zero = jnp.zeros_like(point_weight)
    point = jnp.block([[point_weight, zero], [zero, point_weight]])
    bias = jnp.concatenate([point_bias, point_bias]).reshape(128, 1)
    message = [((512, 128), bf16)]

    (sent,) = call(spectra_kernel, message, field, forward, weave)
    columns = exchange(sent, "grid")

    local = spectral_weight.astype(bf16).reshape(8, 2, C, C).transpose(0, 2, 1, 3).reshape(512, 128)
    whole = exchange(
        jnp.broadcast_to(local[None], (BLOCKS, 512, 128)).reshape(BLOCKS * 512, 128), "dp"
    )

    modes, sent = call(
        forward_modes_kernel, [((128, 128), bf16)] + message, columns, whole, to_modes, to_rows
    )
    received = exchange(sent, "grid")
    pre_grad, sent = call(
        slope_kernel,
        [((512, 512), bf16)] + message,
        received,
        field,
        cotangent,
        point.T,
        bias,
        inverse,
        weave,
    )
    columns = exchange(sent, "grid")
    pair, sent = call(
        backward_modes_kernel,
        [((128, 128), bf16)] + message,
        columns,
        whole,
        modes,
        to_modes,
        to_rows,
    )
    pair = exchange(pair, "dp")
    received = exchange(sent, "grid")
    flat = (16, C * C)
    new_weight, new_first, new_second = call(
        adam_kernel,
        [(flat, f32)] * 3,
        pair,
        pick,
        spectral_weight.reshape(flat),
        first_moment.reshape(flat),
        second_moment.reshape(flat),
    )
    (grad_field,) = call(
        field_kernel, [((512, 512), bf16)], received, pre_grad, point, forward, weave
    )
    shape = spectral_weight.shape
    return (
        grad_field.reshape(in_field.shape),
        new_weight.reshape(shape),
        new_first.reshape(shape),
        new_second.reshape(shape),
    )


def solution(mesh):
    split = P("dp", "grid", None, None)
    return jax.shard_map(
        shards,
        mesh=mesh,
        in_specs=(split, split, P(), P(), split, split, split),
        out_specs=(split, split, split, split),
        check_vma=False,
    )
```

```python
import math

import jax
import jax.numpy as jnp
import numpy as np
from jax import lax
from jax.experimental import pallas as pl
from jax.experimental.pallas import tpu as pltpu
from jax.sharding import PartitionSpec as P

C = 64
NX = 512
NY = 512
MX = 64
MY = 64
SLAB = 8
QUAD = 4
HALF = 64
BLOCKS = 8

beta_one = 0.9
beta_two = 0.999
learn_rate = 0.01
adam_step = 100
epsilon_adam = 1e-08

f32 = jnp.float32
bf16 = jnp.bfloat16


def tables():
    frequency = np.arange(MY)
    position = np.arange(NY)
    angles = ((position[:, None] * frequency[None, :]) % NY).astype(np.float32) * np.float32(
        2.0 * math.pi / NY
    )
    cos, sin = np.cos(angles), np.sin(angles)
    forward = np.stack([cos, -sin], axis=-1).reshape(NY, 2 * MY).T
    factor = np.where(frequency == 0, 1.0, 2.0).astype(np.float32) / np.float32(NX * NY)
    inverse = np.stack([factor * cos, -factor * sin], axis=-1).reshape(NY, 2 * MY).T

    column = np.arange(MX)
    wavenumber = np.where(column < MX // 2, column, NX - MX + column)
    rows = np.arange(NX)
    turn = ((wavenumber[:, None] * rows[None, :]) % NX).astype(np.float32) * np.float32(
        2.0 * math.pi / NX
    )
    col_cos, col_sin = np.cos(turn), np.sin(turn)

    by_slab = lambda t: t.reshape(BLOCKS, 8, NX // SLAB, QUAD, 2)
    c, s = by_slab(col_cos), by_slab(col_sin)
    to_modes = np.stack([np.stack([c, s], 0), np.stack([-s, c], 0)], 0)
    to_modes = to_modes.transpose(6, 2, 0, 3, 4, 1, 5).reshape(256, 512)

    by_slab = lambda t: t.reshape(MX, NX // SLAB, QUAD, 2)
    c, s = by_slab(col_cos), by_slab(col_sin)
    to_rows = np.stack([np.stack([c, -s], 0), np.stack([s, c], 0)], 0)
    to_rows = to_rows.transpose(3, 0, 4, 1, 5, 2).reshape(512, 256)

    pick = np.zeros((4, 8, 8, 2, 8, 2, 8), np.float32)
    for b in range(8):
        for j in range(8):
            for p in range(2):
                pick[0, b, j, p, b, 0, j] = 1.0
                pick[1, b, j, p, b, 1, j] = 1.0
                pick[2, b, j, p, b, p, j] = 1.0
                pick[3, b, j, p, b, 1 - p, j] = 1.0 - 2.0 * p
    pick = pick.reshape(512, 128)
    made = (forward, inverse, to_modes, to_rows, pick)
    return tuple(np.asarray(t, np.float32).astype(jnp.bfloat16) for t in made)


def mm(a, b):
    return lax.dot_general(a, b, (((1,), (0,)), ((), ())), preferred_element_type=f32)


def mm_nt(a, b):
    return lax.dot_general(a, b, (((1,), (1,)), ((), ())), preferred_element_type=f32)


def mm_tn(a, b):
    return lax.dot_general(a, b, (((0,), (0,)), ((), ())), preferred_element_type=f32)


def low_lanes(shape):
    return lax.broadcasted_iota(jnp.int32, shape, len(shape) - 1) % 128 < HALF


def swap(value):
    return jnp.concatenate([value[:, HALF:], value[:, :HALF]], axis=1)


def part(q):
    return slice(q * 128, (q + 1) * 128)


def quarter(q):
    return pl.ds(q, 128, stride=QUAD)


def modes_of(received, to_modes):
    both = mm(to_modes, received)
    chosen = jnp.where(low_lanes((128, 128)), both[:128], both[128:])
    return (chosen + swap(chosen)).astype(bf16)


def rows_of(modes, to_rows):
    low = low_lanes((MX, 128))
    turned = swap(modes)
    stacked = jnp.concatenate(
        [
            jnp.where(low, modes, 0.0),
            jnp.where(low, 0.0, turned),
            jnp.where(low, turned, 0.0),
            jnp.where(low, 0.0, modes),
        ],
        axis=0,
    ).astype(bf16)
    return mm(to_rows, stacked).astype(bf16)


def own_block(shape):
    return (
        lax.broadcasted_iota(jnp.int32, shape, 0) % 8
        == lax.broadcasted_iota(jnp.int32, shape, 1) // HALF
    )


def gelu_slope(value):
    return 0.5 * (1.0 + lax.erf(value / math.sqrt(2.0))) + value * jnp.exp(
        -0.5 * value * value
    ) / math.sqrt(2.0 * math.pi)


def spectra_kernel(field_hbm, table_hbm, out_ref, field_ref, table_ref, woven_ref, sems):
    table_copy = pltpu.make_async_copy(table_hbm, table_ref, sems.at[QUAD])
    table_copy.start()
    copies = [
        pltpu.make_async_copy(field_hbm.at[part(q)], field_ref.at[part(q)], sems.at[q])
        for q in range(QUAD)
    ]
    for copy in copies:
        copy.start()
    table_copy.wait()
    table = table_ref[...]
    for q in range(QUAD):
        copies[q].wait()
        woven_ref[quarter(q), :] = mm_nt(table, field_ref[part(q), :])
    out_ref[...] = woven_ref[...].astype(bf16)


def modes_kernel(received_ref, to_modes_ref, modes_ref):
    modes_ref[...] = modes_of(received_ref[...], to_modes_ref[...])


def forward_modes_kernel(modes_ref, weight_ref, to_rows_ref, out_ref):
    wide = modes_ref[...].astype(f32)
    own = own_block((16, 512))
    sign = jnp.where(low_lanes((8, 128)), -1.0, 1.0)
    mixed = []
    for block in range(BLOCKS):
        mine = wide[block * 16 : (block + 1) * 16]
        spread = jnp.where(own, jnp.concatenate([mine] * 4, axis=1), 0.0).astype(bf16)
        product = mm(spread, weight_ref[block * 512 : (block + 1) * 512, :])
        mixed.append(product[:8] + sign * swap(product[8:]))
    out_ref[...] = rows_of(jnp.concatenate(mixed, axis=0), to_rows_ref[...])


def backward_modes_kernel(
    received_ref, weight_ref, modes_ref, to_modes_ref, to_rows_ref, pair_ref, out_ref
):
    grads = modes_of(received_ref[...], to_modes_ref[...])
    wide = grads.astype(f32)
    pair_ref[...] = jnp.where(
        low_lanes((128, 128)), modes_ref[...].astype(f32), wide
    ).astype(bf16)
    own = own_block((16, 512))
    low = low_lanes((8, 128))
    mixed = []
    for block in range(BLOCKS):
        real = wide[block * 16 : block * 16 + 8]
        imaginary = wide[block * 16 + 8 : block * 16 + 16]
        turned = jnp.concatenate(
            [jnp.where(low, real, imaginary), jnp.where(low, imaginary, -real)], axis=0
        ).astype(bf16)
        product = mm_nt(turned, weight_ref[block * 512 : (block + 1) * 512, :])
        product = jnp.where(own, product, 0.0)
        folded = product[:, :128] + product[:, 128:256] + product[:, 256:384] + product[:, 384:]
        folded = folded + swap(folded)
        mixed.append(jnp.where(low, folded[:8], folded[8:]))
    out_ref[...] = rows_of(jnp.concatenate(mixed, axis=0), to_rows_ref[...])


def slope_kernel(
    received_ref,
    field_hbm,
    cotangent_hbm,
    point_ref,
    bias_ref,
    inverse_ref,
    grad_ref,
    out_ref,
    field_ref,
    cotangent_ref,
    woven_ref,
    sems,
):
    copies = []
    for q in range(QUAD):
        for n, (source, target) in enumerate(
            ((field_hbm, field_ref), (cotangent_hbm, cotangent_ref))
        ):
            copy = pltpu.make_async_copy(
                source.at[part(q)], target.at[part(q)], sems.at[2 * q + n]
            )
            copy.start()
            copies.append(copy)
    inverse = inverse_ref[...]
    woven_ref[...] = received_ref[...].astype(f32)
    rows = [woven_ref[quarter(q), :].astype(bf16) for q in range(QUAD)]
    for q in range(QUAD):
        copies[2 * q].wait()
        value = mm_tn(rows[q], inverse) + mm(point_ref[...], field_ref[part(q), :])
        value = value + bias_ref[...]
        copies[2 * q + 1].wait()
        grad = (cotangent_ref[part(q), :].astype(f32) * gelu_slope(value)).astype(bf16)
        grad_ref[part(q), :] = grad
        woven_ref[quarter(q), :] = mm_nt(inverse, grad)
    out_ref[...] = woven_ref[...].astype(bf16)


def field_kernel(
    received_ref, grad_ref, point_ref, forward_ref, out_hbm, out_ref, woven_ref, sems
):
    forward = forward_ref[...]
    woven_ref[...] = received_ref[...].astype(f32)
    copies = []
    for q in range(QUAD):
        rows = woven_ref[quarter(q), :].astype(bf16)
        value = mm_tn(rows, forward) + mm(point_ref[...], grad_ref[part(q), :])
        out_ref[part(q), :] = value.astype(bf16)
        copy = pltpu.make_async_copy(out_ref.at[part(q)], out_hbm.at[part(q)], sems.at[q])
        copy.start()
        copies.append(copy)
    for copy in copies:
        copy.wait()


def adam_kernel(
    pair_ref, pick_ref, weight_ref, first_ref, second_ref, new_weight_ref, new_first_ref, new_second_ref
):
    width = 512
    bias_one = 1.0 - beta_one**adam_step
    bias_two = 1.0 - beta_two**adam_step
    picked = mm(pick_ref[...], pair_ref[...]).astype(bf16)
    row = lax.broadcasted_iota(jnp.int32, (128, width), 0)
    lane = lax.broadcasted_iota(jnp.int32, (128, width), 1)
    outer = jnp.where(row == HALF + lane % HALF, 1.0, 0.0).astype(bf16)
    right_one = mm(picked[256:384], outer)
    right_two = mm(picked[384:], outer)
    for n in range(C * C // width):
        inner = jnp.where(row == n * (width // HALF) + lane // HALF, 1.0, 0.0).astype(bf16)
        product = mm(picked[:128], inner) * right_one + mm(picked[128:256], inner) * right_two
        gradient = product[:16]
        for b in range(1, 8):
            gradient = gradient + product[b * 16 : (b + 1) * 16]
        at = slice(n * width, (n + 1) * width)
        first = beta_one * first_ref[:, at] + (1.0 - beta_one) * gradient
        second = beta_two * second_ref[:, at] + (1.0 - beta_two) * gradient * gradient
        new_first_ref[:, at] = first
        new_second_ref[:, at] = second
        step = learn_rate * (first / bias_one) / (jnp.sqrt(second / bias_two) + epsilon_adam)
        new_weight_ref[:, at] = weight_ref[:, at] - step


HBM = pl.BlockSpec(memory_space=pl.ANY)
VMEM = pl.BlockSpec(memory_space=pltpu.VMEM)


def call(kernel, outs, *arrays, scratch=(), far=(), far_out=False):
    return pl.pallas_call(
        kernel,
        out_shape=[jax.ShapeDtypeStruct(shape, dtype) for shape, dtype in outs],
        in_specs=[HBM if n in far else VMEM for n in range(len(arrays))],
        out_specs=[HBM if far_out else VMEM for _ in outs],
        scratch_shapes=list(scratch),
        compiler_params=pltpu.CompilerParams(vmem_limit_bytes=40 * 1024 * 1024),
    )(*arrays)


def exchange(array, axis):
    return lax.all_to_all(array, axis, split_axis=0, concat_axis=0, tiled=True)


def shards(
    in_field, out_grad, point_weight, point_bias, spectral_weight, first_moment, second_moment
):
    forward, inverse, to_modes, to_rows, pick = (jnp.asarray(t) for t in tables())
    field = in_field.reshape(SLAB * C, NY)
    cotangent = out_grad.reshape(SLAB * C, NY)
    zero = jnp.zeros_like(point_weight)
    point = jnp.block([[point_weight, zero], [zero, point_weight]])
    bias = jnp.concatenate([point_bias, point_bias]).reshape(128, 1)
    message = [((512, 128), bf16)]

    plane = pltpu.VMEM((512, 512), bf16)
    woven = pltpu.VMEM((512, 128), f32)
    dma = pltpu.SemaphoreType.DMA

    (sent,) = call(
        spectra_kernel,
        message,
        field,
        forward,
        far=(0, 1),
        scratch=(plane, pltpu.VMEM((128, 512), bf16), woven, dma((QUAD + 1,))),
    )
    columns = exchange(sent, "grid")

    local = spectral_weight.astype(bf16).reshape(8, 2, C, C).transpose(0, 2, 1, 3).reshape(512, 128)
    whole = exchange(
        jnp.broadcast_to(local[None], (BLOCKS, 512, 128)).reshape(BLOCKS * 512, 128), "dp"
    )

    (modes,) = call(modes_kernel, [((128, 128), bf16)], columns, to_modes)
    (sent,) = call(forward_modes_kernel, message, modes, whole, to_rows)
    received = exchange(sent, "grid")
    pre_grad, sent = call(
        slope_kernel,
        [((512, 512), bf16)] + message,
        received,
        field,
        cotangent,
        point.T,
        bias,
        inverse,
        far=(1, 2),
        scratch=(plane, plane, woven, dma((2 * QUAD,))),
    )
    columns = exchange(sent, "grid")
    pair, sent = call(
        backward_modes_kernel,
        [((128, 128), bf16)] + message,
        columns,
        whole,
        modes,
        to_modes,
        to_rows,
    )
    pair = exchange(pair, "dp")
    received = exchange(sent, "grid")
    flat = (16, C * C)
    new_weight, new_first, new_second = call(
        adam_kernel,
        [(flat, f32)] * 3,
        pair,
        pick,
        spectral_weight.reshape(flat),
        first_moment.reshape(flat),
        second_moment.reshape(flat),
    )
    (grad_field,) = call(
        field_kernel,
        [((512, 512), bf16)],
        received,
        pre_grad,
        point,
        forward,
        far_out=True,
        scratch=(plane, woven, dma((QUAD,))),
    )
    shape = spectral_weight.shape
    return (
        grad_field.reshape(in_field.shape),
        new_weight.reshape(shape),
        new_first.reshape(shape),
        new_second.reshape(shape),
    )


def solution(mesh):
    split = P("dp", "grid", None, None)
    return jax.shard_map(
        shards,
        mesh=mesh,
        in_specs=(split, split, P(), P(), split, split, split),
        out_specs=(split, split, split, split),
        check_vma=False,
    )
```

```python
import math

import jax
import jax.numpy as jnp
import numpy as np
from jax import lax
from jax.experimental import pallas as pl
from jax.experimental.pallas import tpu as pltpu
from jax.sharding import PartitionSpec as P

C = 64
NX = 512
NY = 512
MX = 64
MY = 64
SLAB = 8
QUAD = 4
HALF = 64
BLOCKS = 8

beta_one = 0.9
beta_two = 0.999
learn_rate = 0.01
adam_step = 100
epsilon_adam = 1e-08

f32 = jnp.float32
bf16 = jnp.bfloat16


def tables():
    frequency = np.arange(MY)
    position = np.arange(NY)
    angles = ((position[:, None] * frequency[None, :]) % NY).astype(np.float32) * np.float32(
        2.0 * math.pi / NY
    )
    cos, sin = np.cos(angles), np.sin(angles)
    forward = np.stack([cos, -sin], axis=-1).reshape(NY, 2 * MY).T
    factor = np.where(frequency == 0, 1.0, 2.0).astype(np.float32) / np.float32(NX * NY)
    inverse = np.stack([factor * cos, -factor * sin], axis=-1).reshape(NY, 2 * MY).T

    column = np.arange(MX)
    wavenumber = np.where(column < MX // 2, column, NX - MX + column)
    rows = np.arange(NX)
    turn = ((wavenumber[:, None] * rows[None, :]) % NX).astype(np.float32) * np.float32(
        2.0 * math.pi / NX
    )
    col_cos, col_sin = np.cos(turn), np.sin(turn)

    by_slab = lambda t: t.reshape(BLOCKS, 8, NX // SLAB, QUAD, 2)
    c, s = by_slab(col_cos), by_slab(col_sin)
    to_modes = np.stack([np.stack([c, s], 0), np.stack([-s, c], 0)], 0)
    to_modes = to_modes.transpose(6, 2, 0, 3, 4, 1, 5).reshape(256, 512)

    by_slab = lambda t: t.reshape(MX, NX // SLAB, QUAD, 2)
    c, s = by_slab(col_cos), by_slab(col_sin)
    to_rows = np.stack([np.stack([c, -s], 0), np.stack([s, c], 0)], 0)
    to_rows = to_rows.transpose(3, 0, 4, 1, 5, 2).reshape(512, 256)

    pick = np.zeros((4, 8, 8, 2, 8, 2, 8), np.float32)
    for b in range(8):
        for j in range(8):
            for p in range(2):
                pick[0, b, j, p, b, 0, j] = 1.0
                pick[1, b, j, p, b, 1, j] = 1.0
                pick[2, b, j, p, b, p, j] = 1.0
                pick[3, b, j, p, b, 1 - p, j] = 1.0 - 2.0 * p
    pick = pick.reshape(512, 128)
    made = (forward, inverse, to_modes, to_rows, pick)
    return tuple(np.asarray(t, np.float32).astype(jnp.bfloat16) for t in made)


def mm(a, b):
    return lax.dot_general(a, b, (((1,), (0,)), ((), ())), preferred_element_type=f32)


def mm_nt(a, b):
    return lax.dot_general(a, b, (((1,), (1,)), ((), ())), preferred_element_type=f32)


def mm_tn(a, b):
    return lax.dot_general(a, b, (((0,), (0,)), ((), ())), preferred_element_type=f32)


def low_lanes(shape):
    return lax.broadcasted_iota(jnp.int32, shape, len(shape) - 1) % 128 < HALF


def swap(value):
    return jnp.concatenate([value[:, HALF:], value[:, :HALF]], axis=1)


def part(q):
    return slice(q * 128, (q + 1) * 128)


def quarter(q):
    return pl.ds(q, 128, stride=QUAD)


def modes_of(received, to_modes):
    both = mm(to_modes, received)
    chosen = jnp.where(low_lanes((128, 128)), both[:128], both[128:])
    return (chosen + swap(chosen)).astype(bf16)


def rows_of(modes, to_rows):
    low = low_lanes((MX, 128))
    turned = swap(modes)
    stacked = jnp.concatenate(
        [
            jnp.where(low, modes, 0.0),
            jnp.where(low, 0.0, turned),
            jnp.where(low, turned, 0.0),
            jnp.where(low, 0.0, modes),
        ],
        axis=0,
    ).astype(bf16)
    return mm(to_rows, stacked).astype(bf16)


def own_block(shape):
    return (
        lax.broadcasted_iota(jnp.int32, shape, 0) % 8
        == lax.broadcasted_iota(jnp.int32, shape, 1) // HALF
    )


def gelu_slope(value):
    return 0.5 * (1.0 + lax.erf(value / math.sqrt(2.0))) + value * jnp.exp(
        -0.5 * value * value
    ) / math.sqrt(2.0 * math.pi)


def spectra_kernel(field_hbm, table_hbm, out_ref, field_ref, table_ref, woven_ref, sems):
    table_copy = pltpu.make_async_copy(table_hbm, table_ref, sems.at[QUAD])
    table_copy.start()
    copies = [
        pltpu.make_async_copy(field_hbm.at[part(q)], field_ref.at[part(q)], sems.at[q])
        for q in range(QUAD)
    ]
    for copy in copies:
        copy.start()
    table_copy.wait()
    table = table_ref[...]
    for q in range(QUAD):
        copies[q].wait()
        woven_ref[quarter(q), :] = mm_nt(table, field_ref[part(q), :])
    out_ref[...] = woven_ref[...].astype(bf16)


def copies_kernel(local_ref, out_ref):
    for block in range(BLOCKS):
        out_ref[block * 512 : (block + 1) * 512, :] = local_ref[...]


def modes_kernel(received_ref, to_modes_ref, modes_ref):
    modes_ref[...] = modes_of(received_ref[...], to_modes_ref[...])


def forward_modes_kernel(modes_ref, weight_ref, to_rows_ref, out_ref):
    wide = modes_ref[...].astype(f32)
    own = own_block((16, 512))
    sign = jnp.where(low_lanes((8, 128)), -1.0, 1.0)
    mixed = []
    for block in range(BLOCKS):
        mine = wide[block * 16 : (block + 1) * 16]
        spread = jnp.where(own, jnp.concatenate([mine] * 4, axis=1), 0.0).astype(bf16)
        product = mm(spread, weight_ref[block * 512 : (block + 1) * 512, :])
        mixed.append(product[:8] + sign * swap(product[8:]))
    out_ref[...] = rows_of(jnp.concatenate(mixed, axis=0), to_rows_ref[...])


def backward_modes_kernel(
    received_ref, weight_ref, modes_ref, to_modes_ref, to_rows_ref, pair_ref, out_ref
):
    grads = modes_of(received_ref[...], to_modes_ref[...])
    wide = grads.astype(f32)
    pair_ref[...] = jnp.where(
        low_lanes((128, 128)), modes_ref[...].astype(f32), wide
    ).astype(bf16)
    own = own_block((16, 512))
    low = low_lanes((8, 128))
    mixed = []
    for block in range(BLOCKS):
        real = wide[block * 16 : block * 16 + 8]
        imaginary = wide[block * 16 + 8 : block * 16 + 16]
        turned = jnp.concatenate(
            [jnp.where(low, real, imaginary), jnp.where(low, imaginary, -real)], axis=0
        ).astype(bf16)
        product = mm_nt(turned, weight_ref[block * 512 : (block + 1) * 512, :])
        product = jnp.where(own, product, 0.0)
        folded = product[:, :128] + product[:, 128:256] + product[:, 256:384] + product[:, 384:]
        folded = folded + swap(folded)
        mixed.append(jnp.where(low, folded[:8], folded[8:]))
    out_ref[...] = rows_of(jnp.concatenate(mixed, axis=0), to_rows_ref[...])


def linear_kernel(field_ref, cotangent_hbm, point_ref, bias_ref, out_ref, cotangent_ref, sems):
    copy = pltpu.make_async_copy(cotangent_hbm, cotangent_ref, sems.at[0])
    copy.start()
    for q in range(QUAD):
        out_ref[part(q), :] = mm(point_ref[...], field_ref[part(q), :]) + bias_ref[...]
    copy.wait()


def slope_kernel(
    received_ref, linear_ref, cotangent_ref, inverse_ref, grad_ref, out_ref, woven_ref
):
    inverse = inverse_ref[...]
    woven_ref[...] = received_ref[...].astype(f32)
    rows = [woven_ref[quarter(q), :].astype(bf16) for q in range(QUAD)]
    for q in range(QUAD):
        value = mm_tn(rows[q], inverse) + linear_ref[part(q), :]
        grad = (cotangent_ref[part(q), :].astype(f32) * gelu_slope(value)).astype(bf16)
        grad_ref[part(q), :] = grad
        woven_ref[quarter(q), :] = mm_nt(inverse, grad)
    out_ref[...] = woven_ref[...].astype(bf16)


def field_kernel(
    received_ref,
    grad_ref,
    point_ref,
    forward_ref,
    weight_hbm,
    first_hbm,
    second_hbm,
    out_hbm,
    weight_out,
    first_out,
    second_out,
    out_ref,
    woven_ref,
    masters_ref,
    sems,
):
    loads = []
    for n, source in enumerate((weight_hbm, first_hbm, second_hbm)):
        copy = pltpu.make_async_copy(source, masters_ref.at[n], sems.at[QUAD + n])
        copy.start()
        loads.append(copy)
    forward = forward_ref[...]
    woven_ref[...] = received_ref[...].astype(f32)
    copies = []
    for q in range(QUAD):
        rows = woven_ref[quarter(q), :].astype(bf16)
        value = mm_tn(rows, forward) + mm(point_ref[...], grad_ref[part(q), :])
        out_ref[part(q), :] = value.astype(bf16)
        copy = pltpu.make_async_copy(out_ref.at[part(q)], out_hbm.at[part(q)], sems.at[q])
        copy.start()
        copies.append(copy)
    for n, target in enumerate((weight_out, first_out, second_out)):
        loads[n].wait()
        for j in range(8):
            target[2 * j : 2 * j + 2, :] = masters_ref[n, j, 0]
    for copy in copies:
        copy.wait()


def adam_kernel(
    pair_ref, pick_ref, weight_ref, first_ref, second_ref, new_weight_ref, new_first_ref, new_second_ref
):
    width = 512
    bias_one = 1.0 - beta_one**adam_step
    bias_two = 1.0 - beta_two**adam_step
    picked = mm(pick_ref[...], pair_ref[...]).astype(bf16)
    row = lax.broadcasted_iota(jnp.int32, (128, width), 0)
    lane = lax.broadcasted_iota(jnp.int32, (128, width), 1)
    outer = jnp.where(row == HALF + lane % HALF, 1.0, 0.0).astype(bf16)
    right_one = mm(picked[256:384], outer)
    right_two = mm(picked[384:], outer)
    for n in range(C * C // width):
        inner = jnp.where(row == n * (width // HALF) + lane // HALF, 1.0, 0.0).astype(bf16)
        product = mm(picked[:128], inner) * right_one + mm(picked[128:256], inner) * right_two
        gradient = product[:16]
        for b in range(1, 8):
            gradient = gradient + product[b * 16 : (b + 1) * 16]
        at = slice(n * width, (n + 1) * width)
        first = beta_one * first_ref[:, at] + (1.0 - beta_one) * gradient
        second = beta_two * second_ref[:, at] + (1.0 - beta_two) * gradient * gradient
        step = learn_rate * (first / bias_one) / (jnp.sqrt(second / bias_two) + epsilon_adam)
        weight = weight_ref[:, at] - step
        for j in range(8):
            rows = slice(2 * j, 2 * j + 2)
            new_weight_ref[j, 0, :, at] = weight[rows]
            new_first_ref[j, 0, :, at] = first[rows]
            new_second_ref[j, 0, :, at] = second[rows]


HBM = pl.BlockSpec(memory_space=pltpu.HBM)
VMEM = pl.BlockSpec(memory_space=pltpu.VMEM)


def call(kernel, outs, *arrays, scratch=(), far=(), far_out=(), near_out=False):
    arrays = [
        pltpu.with_memory_space_constraint(a, pltpu.HBM) if n in far else a
        for n, a in enumerate(arrays)
    ]
    place = pltpu.VMEM if near_out else jax.ShapeDtypeStruct
    return pl.pallas_call(
        kernel,
        out_shape=[place(shape, dtype) for shape, dtype in outs],
        in_specs=[HBM if n in far else VMEM for n in range(len(arrays))],
        out_specs=[HBM if n in far_out else VMEM for n in range(len(outs))],
        scratch_shapes=list(scratch),
        compiler_params=pltpu.CompilerParams(vmem_limit_bytes=24 * 1024 * 1024),
    )(*arrays)


def exchange(array, axis):
    return lax.all_to_all(array, axis, split_axis=0, concat_axis=0, tiled=True)


def shards(
    in_field, out_grad, point_weight, point_bias, spectral_weight, first_moment, second_moment
):
    forward, inverse, to_modes, to_rows, pick = (jnp.asarray(t) for t in tables())
    field = in_field.reshape(SLAB * C, NY)
    cotangent = out_grad.reshape(SLAB * C, NY)
    zero = jnp.zeros_like(point_weight)
    point = jnp.block([[point_weight, zero], [zero, point_weight]])
    bias = jnp.concatenate([point_bias, point_bias]).reshape(128, 1)
    message = [((512, 128), bf16)]

    plane = pltpu.VMEM((512, 512), bf16)
    woven = pltpu.VMEM((512, 128), f32)
    dma = pltpu.SemaphoreType.DMA

    (sent,) = call(
        spectra_kernel,
        message,
        field,
        forward,
        far=(0, 1),
        scratch=(plane, pltpu.VMEM((128, 512), bf16), woven, dma((QUAD + 1,))),
    )
    columns = exchange(sent, "grid")

    local = spectral_weight.astype(bf16).reshape(8, 2, C, C).transpose(0, 2, 1, 3).reshape(512, 128)
    (copies,) = call(copies_kernel, [((BLOCKS * 512, 128), bf16)], local, near_out=True)
    whole = exchange(copies, "dp")

    (modes,) = call(modes_kernel, [((128, 128), bf16)], columns, to_modes)
    linear, near = call(
        linear_kernel,
        [((512, 512), f32), ((512, 512), bf16)],
        field,
        cotangent,
        point.T,
        bias,
        far=(1,),
        scratch=(dma((1,)),),
        near_out=True,
    )
    modes, linear, near = lax.optimization_barrier((modes, linear, near))
    (sent,) = call(forward_modes_kernel, message, modes, whole, to_rows)
    received = exchange(sent, "grid")
    pre_grad, sent = call(
        slope_kernel,
        [((512, 512), bf16)] + message,
        received,
        linear,
        near,
        inverse,
        scratch=(woven,),
    )
    columns = exchange(sent, "grid")
    pair, sent = call(
        backward_modes_kernel,
        [((128, 128), bf16)] + message,
        columns,
        whole,
        modes,
        to_modes,
        to_rows,
    )
    received, pair = lax.optimization_barrier((exchange(sent, "grid"), pair))
    pair = exchange(pair, "dp")
    masters = (spectral_weight, first_moment, second_moment)
    shape = spectral_weight.shape
    grad_field, *flat = call(
        field_kernel,
        [((512, 512), bf16)] + [((16, C * C), f32)] * 3,
        received,
        pre_grad,
        point,
        forward,
        *masters,
        far=(4, 5, 6),
        far_out=(0,),
        scratch=(plane, woven, pltpu.VMEM((3,) + shape, f32), dma((QUAD + 3,))),
    )
    new_weight, new_first, new_second = call(adam_kernel, [(shape, f32)] * 3, pair, pick, *flat)
    return (grad_field.reshape(in_field.shape), new_weight, new_first, new_second)


def solution(mesh):
    split = P("dp", "grid", None, None)
    return jax.shard_map(
        shards,
        mesh=mesh,
        in_specs=(split, split, P(), P(), split, split, split),
        out_specs=(split, split, split, split),
        check_vma=False,
    )
```

```python
import math

import jax
import jax.numpy as jnp
import numpy as np
from jax import lax
from jax.experimental import pallas as pl
from jax.experimental.pallas import tpu as pltpu
from jax.sharding import PartitionSpec as P

C = 64
NX = 512
NY = 512
MX = 64
MY = 64
SLAB = 8
QUAD = 4
HALF = 64
BLOCKS = 8

GRID_ORDER = [(52 + 27 * k) % 64 for k in range(64)]
DP_ORDER = [(k + 5) % 8 for k in range(8)]

beta_one = 0.9
beta_two = 0.999
learn_rate = 0.01
adam_step = 100
epsilon_adam = 1e-08

f32 = jnp.float32
bf16 = jnp.bfloat16


def tables():
    frequency = np.array(GRID_ORDER)
    position = np.arange(NY)
    angles = ((position[:, None] * frequency[None, :]) % NY).astype(np.float32) * np.float32(
        2.0 * math.pi / NY
    )
    cos, sin = np.cos(angles), np.sin(angles)
    forward = np.stack([cos, -sin], axis=-1).reshape(NY, 2 * MY).T
    factor = np.where(frequency == 0, 1.0, 2.0).astype(np.float32) / np.float32(NX * NY)
    inverse = np.stack([factor * cos, -factor * sin], axis=-1).reshape(NY, 2 * MY).T

    column = np.arange(MX)
    wavenumber = np.where(column < MX // 2, column, NX - MX + column)
    rows = np.arange(NX)
    turn = ((wavenumber[:, None] * rows[None, :]) % NX).astype(np.float32) * np.float32(
        2.0 * math.pi / NX
    )
    by_order = lambda t: (
        t.reshape(BLOCKS, 8, NX // SLAB, SLAB)[DP_ORDER][:, :, GRID_ORDER].reshape(MX, NX)
    )
    col_cos, col_sin = by_order(np.cos(turn)), by_order(np.sin(turn))

    by_slab = lambda t: t.reshape(BLOCKS, 8, NX // SLAB, QUAD, 2)
    c, s = by_slab(col_cos), by_slab(col_sin)
    to_modes = np.stack([np.stack([c, s], 0), np.stack([-s, c], 0)], 0)
    to_modes = to_modes.transpose(6, 2, 0, 3, 4, 1, 5).reshape(256, 512)

    by_slab = lambda t: t.reshape(MX, NX // SLAB, QUAD, 2)
    c, s = by_slab(col_cos), by_slab(col_sin)
    to_rows = np.stack([np.stack([c, -s], 0), np.stack([s, c], 0)], 0)
    to_rows = to_rows.transpose(3, 0, 4, 1, 5, 2).reshape(512, 256)

    pick = np.zeros((4, 8, 8, 2, 8, 2, 8), np.float32)
    for b in range(8):
        for j in range(8):
            for p in range(2):
                pick[0, b, j, p, b, 0, j] = 1.0
                pick[1, b, j, p, b, 1, j] = 1.0
                pick[2, b, j, p, b, p, j] = 1.0
                pick[3, b, j, p, b, 1 - p, j] = 1.0 - 2.0 * p
    pick = pick.reshape(512, 128)
    made = (forward, inverse, to_modes, to_rows, pick)
    return tuple(np.asarray(t, np.float32).astype(jnp.bfloat16) for t in made)


def mm(a, b):
    return lax.dot_general(a, b, (((1,), (0,)), ((), ())), preferred_element_type=f32)


def mm_nt(a, b):
    return lax.dot_general(a, b, (((1,), (1,)), ((), ())), preferred_element_type=f32)


def mm_tn(a, b):
    return lax.dot_general(a, b, (((0,), (0,)), ((), ())), preferred_element_type=f32)


def low_lanes(shape):
    return lax.broadcasted_iota(jnp.int32, shape, len(shape) - 1) % 128 < HALF


def swap(value):
    return jnp.concatenate([value[:, HALF:], value[:, :HALF]], axis=1)


def part(q):
    return slice(q * 128, (q + 1) * 128)


def quarter(q):
    return pl.ds(q, 128, stride=QUAD)


def modes_of(received, to_modes):
    both = mm(to_modes, received)
    chosen = jnp.where(low_lanes((128, 128)), both[:128], both[128:])
    return (chosen + swap(chosen)).astype(bf16)


def rows_of(modes, to_rows):
    low = low_lanes((MX, 128))
    turned = swap(modes)
    stacked = jnp.concatenate(
        [
            jnp.where(low, modes, 0.0),
            jnp.where(low, 0.0, turned),
            jnp.where(low, turned, 0.0),
            jnp.where(low, 0.0, modes),
        ],
        axis=0,
    ).astype(bf16)
    return mm(to_rows, stacked).astype(bf16)


def own_block(shape):
    return (
        lax.broadcasted_iota(jnp.int32, shape, 0) % 8
        == lax.broadcasted_iota(jnp.int32, shape, 1) // HALF
    )


def gelu_slope(value):
    return 0.5 * (1.0 + lax.erf(value / math.sqrt(2.0))) + value * jnp.exp(
        -0.5 * value * value
    ) / math.sqrt(2.0 * math.pi)


def spectra_kernel(field_hbm, table_hbm, out_ref, field_ref, table_ref, woven_ref, sems):
    table_copy = pltpu.make_async_copy(table_hbm, table_ref, sems.at[QUAD])
    table_copy.start()
    copies = [
        pltpu.make_async_copy(field_hbm.at[part(q)], field_ref.at[part(q)], sems.at[q])
        for q in range(QUAD)
    ]
    for copy in copies:
        copy.start()
    table_copy.wait()
    table = table_ref[...]
    for q in range(QUAD):
        copies[q].wait()
        woven_ref[quarter(q), :] = mm_nt(table, field_ref[part(q), :])
    out_ref[...] = woven_ref[...].astype(bf16)


def copies_kernel(local_ref, out_ref):
    for block in range(BLOCKS):
        out_ref[block * 512 : (block + 1) * 512, :] = local_ref[...]


def modes_kernel(received_ref, to_modes_ref, modes_ref):
    modes_ref[...] = modes_of(received_ref[...], to_modes_ref[...])


def forward_modes_kernel(modes_ref, weight_ref, to_rows_ref, out_ref):
    wide = modes_ref[...].astype(f32)
    own = own_block((16, 512))
    sign = jnp.where(low_lanes((8, 128)), -1.0, 1.0)
    mixed = []
    for block in range(BLOCKS):
        mine = wide[block * 16 : (block + 1) * 16]
        spread = jnp.where(own, jnp.concatenate([mine] * 4, axis=1), 0.0).astype(bf16)
        product = mm(spread, weight_ref[block * 512 : (block + 1) * 512, :])
        mixed.append(product[:8] + sign * swap(product[8:]))
    out_ref[...] = rows_of(jnp.concatenate(mixed, axis=0), to_rows_ref[...])


def backward_modes_kernel(
    received_ref, weight_ref, modes_ref, to_modes_ref, to_rows_ref, pair_ref, out_ref
):
    grads = modes_of(received_ref[...], to_modes_ref[...])
    wide = grads.astype(f32)
    pair_ref[...] = jnp.where(
        low_lanes((128, 128)), modes_ref[...].astype(f32), wide
    ).astype(bf16)
    own = own_block((16, 512))
    low = low_lanes((8, 128))
    mixed = []
    for block in range(BLOCKS):
        real = wide[block * 16 : block * 16 + 8]
        imaginary = wide[block * 16 + 8 : block * 16 + 16]
        turned = jnp.concatenate(
            [jnp.where(low, real, imaginary), jnp.where(low, imaginary, -real)], axis=0
        ).astype(bf16)
        product = mm_nt(turned, weight_ref[block * 512 : (block + 1) * 512, :])
        product = jnp.where(own, product, 0.0)
        folded = product[:, :128] + product[:, 128:256] + product[:, 256:384] + product[:, 384:]
        folded = folded + swap(folded)
        mixed.append(jnp.where(low, folded[:8], folded[8:]))
    out_ref[...] = rows_of(jnp.concatenate(mixed, axis=0), to_rows_ref[...])


def linear_kernel(field_ref, cotangent_hbm, point_ref, bias_ref, out_ref, cotangent_ref, sems):
    copy = pltpu.make_async_copy(cotangent_hbm, cotangent_ref, sems.at[0])
    copy.start()
    for q in range(QUAD):
        out_ref[part(q), :] = mm(point_ref[...], field_ref[part(q), :]) + bias_ref[...]
    copy.wait()


def slope_kernel(
    received_ref, linear_ref, cotangent_ref, inverse_ref, grad_ref, out_ref, woven_ref
):
    inverse = inverse_ref[...]
    woven_ref[...] = received_ref[...].astype(f32)
    rows = [woven_ref[quarter(q), :].astype(bf16) for q in range(QUAD)]
    for q in range(QUAD):
        value = mm_tn(rows[q], inverse) + linear_ref[part(q), :]
        grad = (cotangent_ref[part(q), :].astype(f32) * gelu_slope(value)).astype(bf16)
        grad_ref[part(q), :] = grad
        woven_ref[quarter(q), :] = mm_nt(inverse, grad)
    out_ref[...] = woven_ref[...].astype(bf16)


def field_kernel(
    received_ref,
    grad_ref,
    point_ref,
    forward_ref,
    weight_hbm,
    first_hbm,
    second_hbm,
    out_hbm,
    weight_out,
    first_out,
    second_out,
    out_ref,
    woven_ref,
    masters_ref,
    sems,
):
    loads = []
    for n, source in enumerate((weight_hbm, first_hbm, second_hbm)):
        copy = pltpu.make_async_copy(source, masters_ref.at[n], sems.at[QUAD + n])
        copy.start()
        loads.append(copy)
    forward = forward_ref[...]
    woven_ref[...] = received_ref[...].astype(f32)
    copies = []
    for q in range(QUAD):
        rows = woven_ref[quarter(q), :].astype(bf16)
        value = mm_tn(rows, forward) + mm(point_ref[...], grad_ref[part(q), :])
        out_ref[part(q), :] = value.astype(bf16)
        copy = pltpu.make_async_copy(out_ref.at[part(q)], out_hbm.at[part(q)], sems.at[q])
        copy.start()
        copies.append(copy)
    for n, target in enumerate((weight_out, first_out, second_out)):
        loads[n].wait()
        for j in range(8):
            target[2 * j : 2 * j + 2, :] = masters_ref[n, j, 0]
    for copy in copies:
        copy.wait()


def adam_kernel(
    pair_ref, pick_ref, weight_ref, first_ref, second_ref, new_weight_ref, new_first_ref, new_second_ref
):
    width = 512
    bias_one = 1.0 - beta_one**adam_step
    bias_two = 1.0 - beta_two**adam_step
    picked = mm(pick_ref[...], pair_ref[...]).astype(bf16)
    row = lax.broadcasted_iota(jnp.int32, (128, width), 0)
    lane = lax.broadcasted_iota(jnp.int32, (128, width), 1)
    outer = jnp.where(row == HALF + lane % HALF, 1.0, 0.0).astype(bf16)
    right_one = mm(picked[256:384], outer)
    right_two = mm(picked[384:], outer)
    for n in range(C * C // width):
        inner = jnp.where(row == n * (width // HALF) + lane // HALF, 1.0, 0.0).astype(bf16)
        product = mm(picked[:128], inner) * right_one + mm(picked[128:256], inner) * right_two
        gradient = product[:16]
        for b in range(1, 8):
            gradient = gradient + product[b * 16 : (b + 1) * 16]
        at = slice(n * width, (n + 1) * width)
        first = beta_one * first_ref[:, at] + (1.0 - beta_one) * gradient
        second = beta_two * second_ref[:, at] + (1.0 - beta_two) * gradient * gradient
        step = learn_rate * (first / bias_one) / (jnp.sqrt(second / bias_two) + epsilon_adam)
        weight = weight_ref[:, at] - step
        for j in range(8):
            rows = slice(2 * j, 2 * j + 2)
            new_weight_ref[j, 0, :, at] = weight[rows]
            new_first_ref[j, 0, :, at] = first[rows]
            new_second_ref[j, 0, :, at] = second[rows]


HBM = pl.BlockSpec(memory_space=pltpu.HBM)
VMEM = pl.BlockSpec(memory_space=pltpu.VMEM)


def call(kernel, outs, *arrays, scratch=(), far=(), far_out=(), near_out=False):
    arrays = [
        pltpu.with_memory_space_constraint(a, pltpu.HBM) if n in far else a
        for n, a in enumerate(arrays)
    ]
    place = pltpu.VMEM if near_out else jax.ShapeDtypeStruct
    return pl.pallas_call(
        kernel,
        out_shape=[place(shape, dtype) for shape, dtype in outs],
        in_specs=[HBM if n in far else VMEM for n in range(len(arrays))],
        out_specs=[HBM if n in far_out else VMEM for n in range(len(outs))],
        scratch_shapes=list(scratch),
        compiler_params=pltpu.CompilerParams(vmem_limit_bytes=24 * 1024 * 1024),
    )(*arrays)


def exchange(array, axis):
    groups = [GRID_ORDER if axis == "grid" else DP_ORDER]
    return lax.all_to_all(
        array, axis, split_axis=0, concat_axis=0, axis_index_groups=groups, tiled=True
    )


def shards(
    in_field, out_grad, point_weight, point_bias, spectral_weight, first_moment, second_moment
):
    forward, inverse, to_modes, to_rows, pick = (jnp.asarray(t) for t in tables())
    field = in_field.reshape(SLAB * C, NY)
    cotangent = out_grad.reshape(SLAB * C, NY)
    zero = jnp.zeros_like(point_weight)
    point = jnp.block([[point_weight, zero], [zero, point_weight]])
    bias = jnp.concatenate([point_bias, point_bias]).reshape(128, 1)
    message = [((512, 128), bf16)]

    plane = pltpu.VMEM((512, 512), bf16)
    woven = pltpu.VMEM((512, 128), f32)
    dma = pltpu.SemaphoreType.DMA

    (sent,) = call(
        spectra_kernel,
        message,
        field,
        forward,
        far=(0, 1),
        scratch=(plane, pltpu.VMEM((128, 512), bf16), woven, dma((QUAD + 1,))),
    )
    columns = exchange(sent, "grid")

    local = spectral_weight.astype(bf16).reshape(8, 2, C, C).transpose(0, 2, 1, 3).reshape(512, 128)
    (copies,) = call(copies_kernel, [((BLOCKS * 512, 128), bf16)], local, near_out=True)
    whole = exchange(copies, "dp")

    (modes,) = call(modes_kernel, [((128, 128), bf16)], columns, to_modes)
    linear, near = call(
        linear_kernel,
        [((512, 512), f32), ((512, 512), bf16)],
        field,
        cotangent,
        point.T,
        bias,
        far=(1,),
        scratch=(dma((1,)),),
        near_out=True,
    )
    modes, linear, near = lax.optimization_barrier((modes, linear, near))
    (sent,) = call(forward_modes_kernel, message, modes, whole, to_rows)
    received = exchange(sent, "grid")
    pre_grad, sent = call(
        slope_kernel,
        [((512, 512), bf16)] + message,
        received,
        linear,
        near,
        inverse,
        scratch=(woven,),
    )
    columns = exchange(sent, "grid")
    pair, sent = call(
        backward_modes_kernel,
        [((128, 128), bf16)] + message,
        columns,
        whole,
        modes,
        to_modes,
        to_rows,
    )
    received, pair = lax.optimization_barrier((exchange(sent, "grid"), pair))
    pair = exchange(pair, "dp")
    masters = (spectral_weight, first_moment, second_moment)
    shape = spectral_weight.shape
    grad_field, *flat = call(
        field_kernel,
        [((512, 512), bf16)] + [((16, C * C), f32)] * 3,
        received,
        pre_grad,
        point,
        forward,
        *masters,
        far=(4, 5, 6),
        far_out=(0,),
        scratch=(plane, woven, pltpu.VMEM((3,) + shape, f32), dma((QUAD + 3,))),
    )
    new_weight, new_first, new_second = call(adam_kernel, [(shape, f32)] * 3, pair, pick, *flat)
    return (grad_field.reshape(in_field.shape), new_weight, new_first, new_second)


def solution(mesh):
    split = P("dp", "grid", None, None)
    return jax.shard_map(
        shards,
        mesh=mesh,
        in_specs=(split, split, P(), P(), split, split, split),
        out_specs=(split, split, split, split),
        check_vma=False,
    )
```

```python
import math

import jax
import jax.numpy as jnp
import numpy as np
from jax import lax
from jax.experimental import pallas as pl
from jax.experimental.pallas import tpu as pltpu
from jax.sharding import PartitionSpec as P

C = 64
NX = 512
NY = 512
MX = 64
MY = 64
SLAB = 8
QUAD = 4
HALF = 64
BLOCKS = 8

GRID_ORDER = [(52 + 27 * k) % 64 for k in range(64)]
DP_ORDER = [(k + 5) % 8 for k in range(8)]

beta_one = 0.9
beta_two = 0.999
learn_rate = 0.01
adam_step = 100
epsilon_adam = 1e-08

f32 = jnp.float32
bf16 = jnp.bfloat16


def tables():
    frequency = np.array(GRID_ORDER)
    position = np.arange(NY)
    angles = ((position[:, None] * frequency[None, :]) % NY).astype(np.float32) * np.float32(
        2.0 * math.pi / NY
    )
    cos, sin = np.cos(angles), np.sin(angles)
    forward = np.stack([cos, -sin], axis=-1).reshape(NY, 2 * MY).T
    factor = np.where(frequency == 0, 1.0, 2.0).astype(np.float32) / np.float32(NX * NY)
    inverse = np.stack([factor * cos, -factor * sin], axis=-1).reshape(NY, 2 * MY).T

    column = np.arange(MX)
    wavenumber = np.where(column < MX // 2, column, NX - MX + column)
    rows = np.arange(NX)
    turn = ((wavenumber[:, None] * rows[None, :]) % NX).astype(np.float32) * np.float32(
        2.0 * math.pi / NX
    )
    by_order = lambda t: (
        t.reshape(BLOCKS, 8, NX // SLAB, SLAB)[DP_ORDER][:, :, GRID_ORDER].reshape(MX, NX)
    )
    col_cos, col_sin = by_order(np.cos(turn)), by_order(np.sin(turn))

    by_slab = lambda t: t.reshape(BLOCKS, 8, NX // SLAB, QUAD, 2)
    c, s = by_slab(col_cos), by_slab(col_sin)
    to_modes = np.stack([np.stack([c, s], 0), np.stack([-s, c], 0)], 0)
    to_modes = to_modes.transpose(6, 2, 0, 3, 4, 1, 5).reshape(256, 512)

    by_slab = lambda t: t.reshape(MX, NX // SLAB, QUAD, 2)
    c, s = by_slab(col_cos), by_slab(col_sin)
    to_rows = np.stack([np.stack([c, -s], 0), np.stack([s, c], 0)], 0)
    to_rows = to_rows.transpose(3, 0, 4, 1, 5, 2).reshape(512, 256)

    pick = np.zeros((2, 128, 2, C // 2, 2), np.float32)
    for c in range(C):
        for p in range(2):
            pick[p, c, c % 2, c // 2, p] = 1.0
    pick = pick.reshape(256, 128)
    made = (forward, inverse, to_modes, to_rows, pick)
    return tuple(np.asarray(t, np.float32).astype(jnp.bfloat16) for t in made)


def mm(a, b):
    return lax.dot_general(a, b, (((1,), (0,)), ((), ())), preferred_element_type=f32)


def mm_nt(a, b):
    return lax.dot_general(a, b, (((1,), (1,)), ((), ())), preferred_element_type=f32)


def mm_tn(a, b):
    return lax.dot_general(a, b, (((0,), (0,)), ((), ())), preferred_element_type=f32)


def low_lanes(shape):
    return lax.broadcasted_iota(jnp.int32, shape, len(shape) - 1) % 128 < HALF


def swap(value):
    return jnp.concatenate([value[:, HALF:], value[:, :HALF]], axis=1)


def part(q):
    return slice(q * 128, (q + 1) * 128)


def quarter(q):
    return pl.ds(q, 128, stride=QUAD)


def modes_of(received, to_modes):
    both = mm(to_modes, received)
    chosen = jnp.where(low_lanes((128, 128)), both[:128], both[128:])
    return (chosen + swap(chosen)).astype(bf16)


def rows_of(modes, to_rows):
    low = low_lanes((MX, 128))
    turned = swap(modes)
    stacked = jnp.concatenate(
        [
            jnp.where(low, modes, 0.0),
            jnp.where(low, 0.0, turned),
            jnp.where(low, turned, 0.0),
            jnp.where(low, 0.0, modes),
        ],
        axis=0,
    ).astype(bf16)
    return mm(to_rows, stacked).astype(bf16)


def own_block(shape):
    return (
        lax.broadcasted_iota(jnp.int32, shape, 0) % 8
        == lax.broadcasted_iota(jnp.int32, shape, 1) // HALF
    )


def gelu_slope(value):
    return 0.5 * (1.0 + lax.erf(value / math.sqrt(2.0))) + value * jnp.exp(
        -0.5 * value * value
    ) / math.sqrt(2.0 * math.pi)


def spectra_kernel(field_hbm, table_hbm, out_ref, field_ref, table_ref, woven_ref, sems):
    table_copy = pltpu.make_async_copy(table_hbm, table_ref, sems.at[QUAD])
    table_copy.start()
    copies = [
        pltpu.make_async_copy(field_hbm.at[part(q)], field_ref.at[part(q)], sems.at[q])
        for q in range(QUAD)
    ]
    for copy in copies:
        copy.start()
    table_copy.wait()
    table = table_ref[...]
    for q in range(QUAD):
        copies[q].wait()
        woven_ref[quarter(q), :] = mm_nt(table, field_ref[part(q), :])
    out_ref[...] = woven_ref[...].astype(bf16)


def copies_kernel(local_ref, out_ref):
    for block in range(BLOCKS):
        out_ref[block * 512 : (block + 1) * 512, :] = local_ref[...]


def modes_kernel(received_ref, to_modes_ref, modes_ref):
    modes_ref[...] = modes_of(received_ref[...], to_modes_ref[...])


def forward_modes_kernel(modes_ref, weight_ref, to_rows_ref, out_ref):
    wide = modes_ref[...].astype(f32)
    own = own_block((16, 512))
    sign = jnp.where(low_lanes((8, 128)), -1.0, 1.0)
    mixed = []
    for block in range(BLOCKS):
        mine = wide[block * 16 : (block + 1) * 16]
        spread = jnp.where(own, jnp.concatenate([mine] * 4, axis=1), 0.0).astype(bf16)
        product = mm(spread, weight_ref[block * 512 : (block + 1) * 512, :])
        mixed.append(product[:8] + sign * swap(product[8:]))
    out_ref[...] = rows_of(jnp.concatenate(mixed, axis=0), to_rows_ref[...])


def backward_modes_kernel(
    received_ref, weight_ref, modes_ref, to_modes_ref, to_rows_ref, pair_ref, out_ref
):
    grads = modes_of(received_ref[...], to_modes_ref[...])
    wide = grads.astype(f32)
    pair_ref[...] = jnp.where(
        low_lanes((128, 128)), modes_ref[...].astype(f32), wide
    ).astype(bf16)
    own = own_block((16, 512))
    low = low_lanes((8, 128))
    mixed = []
    for block in range(BLOCKS):
        real = wide[block * 16 : block * 16 + 8]
        imaginary = wide[block * 16 + 8 : block * 16 + 16]
        turned = jnp.concatenate(
            [jnp.where(low, real, imaginary), jnp.where(low, imaginary, -real)], axis=0
        ).astype(bf16)
        product = mm_nt(turned, weight_ref[block * 512 : (block + 1) * 512, :])
        product = jnp.where(own, product, 0.0)
        folded = product[:, :128] + product[:, 128:256] + product[:, 256:384] + product[:, 384:]
        folded = folded + swap(folded)
        mixed.append(jnp.where(low, folded[:8], folded[8:]))
    out_ref[...] = rows_of(jnp.concatenate(mixed, axis=0), to_rows_ref[...])


def linear_kernel(field_ref, cotangent_hbm, point_ref, bias_ref, out_ref, cotangent_ref, sems):
    copy = pltpu.make_async_copy(cotangent_hbm, cotangent_ref, sems.at[0])
    copy.start()
    for q in range(QUAD):
        out_ref[part(q), :] = mm(point_ref[...], field_ref[part(q), :]) + bias_ref[...]
    copy.wait()


def slope_kernel(
    received_ref, linear_ref, cotangent_ref, inverse_ref, grad_ref, out_ref, woven_ref
):
    inverse = inverse_ref[...]
    woven_ref[...] = received_ref[...].astype(f32)
    rows = [woven_ref[quarter(q), :].astype(bf16) for q in range(QUAD)]
    for q in range(QUAD):
        value = mm_tn(rows[q], inverse) + linear_ref[part(q), :]
        grad = (cotangent_ref[part(q), :].astype(f32) * gelu_slope(value)).astype(bf16)
        grad_ref[part(q), :] = grad
        woven_ref[quarter(q), :] = mm_nt(inverse, grad)
    out_ref[...] = woven_ref[...].astype(bf16)


def field_kernel(
    received_ref,
    grad_ref,
    point_ref,
    forward_ref,
    weight_hbm,
    first_hbm,
    second_hbm,
    out_hbm,
    weight_out,
    first_out,
    second_out,
    out_ref,
    woven_ref,
    sems,
):
    loads = []
    for n, (source, target) in enumerate(
        ((weight_hbm, weight_out), (first_hbm, first_out), (second_hbm, second_out))
    ):
        copy = pltpu.make_async_copy(source, target, sems.at[QUAD + n])
        copy.start()
        loads.append(copy)
    forward = forward_ref[...]
    woven_ref[...] = received_ref[...].astype(f32)
    copies = []
    for q in range(QUAD):
        rows = woven_ref[quarter(q), :].astype(bf16)
        value = mm_tn(rows, forward) + mm(point_ref[...], grad_ref[part(q), :])
        out_ref[part(q), :] = value.astype(bf16)
        copy = pltpu.make_async_copy(out_ref.at[part(q)], out_hbm.at[part(q)], sems.at[q])
        copy.start()
        copies.append(copy)
    for copy in loads + copies:
        copy.wait()


def adam_kernel(
    pair_ref,
    pick_ref,
    weight_ref,
    first_ref,
    second_ref,
    new_weight_hbm,
    new_first_hbm,
    new_second_hbm,
    made_ref,
    sems,
):
    bias_one = 1.0 - beta_one**adam_step
    bias_two = 1.0 - beta_two**adam_step
    wide = pair_ref[...].astype(f32)
    turned = []
    for sample in range(8):
        turned.append(-wide[sample * 16 + 8 : sample * 16 + 16])
        turned.append(wide[sample * 16 : sample * 16 + 8])
    both = jnp.concatenate([wide, jnp.concatenate(turned, axis=0)], axis=1).astype(bf16)
    left = mm(both, pick_ref[...])
    left = jnp.concatenate([left, swap(left)], axis=0).astype(bf16)
    low = low_lanes((128, 128))
    right = jnp.concatenate([jnp.where(low, swap(wide), 0.0), jnp.where(low, 0.0, wide)], axis=0)
    mode = lax.broadcasted_iota(jnp.int32, (256, 128), 0) % 8
    spread = [jnp.where(mode == j, right, 0.0).astype(bf16) for j in range(8)]
    gradients = mm_tn(left, jnp.concatenate(spread, axis=1))
    copies = []
    for j in range(8):
        at = slice(j * 64, (j + 1) * 64)
        gradient = gradients[:64, j * 128 : (j + 1) * 128]
        first = beta_one * first_ref[at, :] + (1.0 - beta_one) * gradient
        second = beta_two * second_ref[at, :] + (1.0 - beta_two) * gradient * gradient
        step = learn_rate * (first / bias_one) / (jnp.sqrt(second / bias_two) + epsilon_adam)
        made_ref[0, at, :] = weight_ref[at, :] - step
        made_ref[1, at, :] = first
        made_ref[2, at, :] = second
        if j % 2 == 1:
            at = slice((j - 1) * 64, (j + 1) * 64)
            for n, target in enumerate((new_weight_hbm, new_first_hbm, new_second_hbm)):
                copy = pltpu.make_async_copy(
                    made_ref.at[n, at], target.at[at], sems.at[3 * (j // 2) + n]
                )
                copy.start()
                copies.append(copy)
    for copy in copies:
        copy.wait()


HBM = pl.BlockSpec(memory_space=pltpu.HBM)
VMEM = pl.BlockSpec(memory_space=pltpu.VMEM)


def call(kernel, outs, *arrays, scratch=(), far=(), far_out=(), near_out=False):
    arrays = [
        pltpu.with_memory_space_constraint(a, pltpu.HBM) if n in far else a
        for n, a in enumerate(arrays)
    ]
    place = pltpu.VMEM if near_out else jax.ShapeDtypeStruct
    return pl.pallas_call(
        kernel,
        out_shape=[place(shape, dtype) for shape, dtype in outs],
        in_specs=[HBM if n in far else VMEM for n in range(len(arrays))],
        out_specs=[HBM if n in far_out else VMEM for n in range(len(outs))],
        scratch_shapes=list(scratch),
        compiler_params=pltpu.CompilerParams(vmem_limit_bytes=24 * 1024 * 1024),
    )(*arrays)


def exchange(array, axis):
    groups = [GRID_ORDER if axis == "grid" else DP_ORDER]
    return lax.all_to_all(
        array, axis, split_axis=0, concat_axis=0, axis_index_groups=groups, tiled=True
    )


def shards(
    in_field, out_grad, point_weight, point_bias, spectral_weight, first_moment, second_moment
):
    forward, inverse, to_modes, to_rows, pick = (jnp.asarray(t) for t in tables())
    field = in_field.reshape(SLAB * C, NY)
    cotangent = out_grad.reshape(SLAB * C, NY)
    zero = jnp.zeros_like(point_weight)
    point = jnp.block([[point_weight, zero], [zero, point_weight]])
    bias = jnp.concatenate([point_bias, point_bias]).reshape(128, 1)
    message = [((512, 128), bf16)]

    plane = pltpu.VMEM((512, 512), bf16)
    woven = pltpu.VMEM((512, 128), f32)
    dma = pltpu.SemaphoreType.DMA

    (sent,) = call(
        spectra_kernel,
        message,
        field,
        forward,
        far=(0, 1),
        scratch=(plane, pltpu.VMEM((128, 512), bf16), woven, dma((QUAD + 1,))),
    )
    columns = exchange(sent, "grid")

    local = spectral_weight.astype(bf16).reshape(8, 2, C, C).transpose(0, 2, 1, 3).reshape(512, 128)
    (copies,) = call(copies_kernel, [((BLOCKS * 512, 128), bf16)], local, near_out=True)
    whole = exchange(copies, "dp")

    (modes,) = call(modes_kernel, [((128, 128), bf16)], columns, to_modes)
    linear, near = call(
        linear_kernel,
        [((512, 512), f32), ((512, 512), bf16)],
        field,
        cotangent,
        point.T,
        bias,
        far=(1,),
        scratch=(dma((1,)),),
        near_out=True,
    )
    modes, linear, near = lax.optimization_barrier((modes, linear, near))
    (sent,) = call(forward_modes_kernel, message, modes, whole, to_rows)
    received = exchange(sent, "grid")
    pre_grad, sent = call(
        slope_kernel,
        [((512, 512), bf16)] + message,
        received,
        linear,
        near,
        inverse,
        scratch=(woven,),
    )
    columns = exchange(sent, "grid")
    pair, sent = call(
        backward_modes_kernel,
        [((128, 128), bf16)] + message,
        columns,
        whole,
        modes,
        to_modes,
        to_rows,
    )
    received, pair = lax.optimization_barrier((exchange(sent, "grid"), pair))
    pair = exchange(pair, "dp")
    masters = [
        m.reshape(8, 2, C // 2, 128).transpose(0, 2, 1, 3).reshape(512, 128)
        for m in (spectral_weight, first_moment, second_moment)
    ]
    flat = [((512, 128), f32)] * 3
    grad_field, *near = call(
        field_kernel,
        [((512, 512), bf16)] + flat,
        received,
        pre_grad,
        point,
        forward,
        *masters,
        far=(4, 5, 6),
        far_out=(0,),
        scratch=(plane, woven, dma((QUAD + 3,))),
    )
    made = call(
        adam_kernel,
        flat,
        pair,
        pick,
        *near,
        far_out=(0, 1, 2),
        scratch=(pltpu.VMEM((3, 512, 128), f32), dma((12,))),
    )
    new_weight, new_first, new_second = (
        m.reshape(8, C // 2, 2, 128).transpose(0, 2, 1, 3).reshape(spectral_weight.shape)
        for m in made
    )
    return (grad_field.reshape(in_field.shape), new_weight, new_first, new_second)


def solution(mesh):
    split = P("dp", "grid", None, None)
    return jax.shard_map(
        shards,
        mesh=mesh,
        in_specs=(split, split, P(), P(), split, split, split),
        out_specs=(split, split, split, split),
        check_vma=False,
    )
```

```python
import math

import jax
import jax.numpy as jnp
import numpy as np
from jax import lax
from jax.experimental import pallas as pl
from jax.experimental.pallas import tpu as pltpu
from jax.sharding import PartitionSpec as P

C = 64
NX = 512
NY = 512
MX = 64
MY = 64
SLAB = 8
QUAD = 4
HALF = 64
BLOCKS = 8

GRID_ORDER = [(52 + 45 * k) % 64 for k in range(64)]
DP_ORDER = [(5 + 3 * k) % 8 for k in range(8)]

beta_one = 0.9
beta_two = 0.999
learn_rate = 0.01
adam_step = 100
epsilon_adam = 1e-08

f32 = jnp.float32
bf16 = jnp.bfloat16


def tables():
    frequency = np.array(GRID_ORDER)
    position = np.arange(NY)
    angles = ((position[:, None] * frequency[None, :]) % NY).astype(np.float32) * np.float32(
        2.0 * math.pi / NY
    )
    cos, sin = np.cos(angles), np.sin(angles)
    forward = np.stack([cos, -sin], axis=-1).reshape(NY, 2 * MY).T
    factor = np.where(frequency == 0, 1.0, 2.0).astype(np.float32) / np.float32(NX * NY)
    inverse = np.stack([factor * cos, -factor * sin], axis=-1).reshape(NY, 2 * MY).T

    column = np.arange(MX)
    wavenumber = np.where(column < MX // 2, column, NX - MX + column)
    rows = np.arange(NX)
    turn = ((wavenumber[:, None] * rows[None, :]) % NX).astype(np.float32) * np.float32(
        2.0 * math.pi / NX
    )
    by_order = lambda t: (
        t.reshape(BLOCKS, 8, NX // SLAB, SLAB)[DP_ORDER][:, :, GRID_ORDER].reshape(MX, NX)
    )
    col_cos, col_sin = by_order(np.cos(turn)), by_order(np.sin(turn))

    by_slab = lambda t: t.reshape(BLOCKS, 8, NX // SLAB, QUAD, 2)
    c, s = by_slab(col_cos), by_slab(col_sin)
    to_modes = np.stack([np.stack([c, s], 0), np.stack([-s, c], 0)], 0)
    to_modes = to_modes.transpose(6, 2, 0, 3, 4, 1, 5).reshape(256, 512)

    by_slab = lambda t: t.reshape(MX, NX // SLAB, QUAD, 2)
    c, s = by_slab(col_cos), by_slab(col_sin)
    to_rows = np.stack([np.stack([c, -s], 0), np.stack([s, c], 0)], 0)
    to_rows = to_rows.transpose(3, 0, 4, 1, 5, 2).reshape(512, 256)

    pick = np.zeros((2, 128, 2, C // 2, 2), np.float32)
    for c in range(C):
        for p in range(2):
            pick[p, c, c % 2, c // 2, p] = 1.0
    pick = pick.reshape(256, 128)
    made = (forward, inverse, to_modes, to_rows, pick)
    return tuple(np.asarray(t, np.float32).astype(jnp.bfloat16) for t in made)


def mm(a, b):
    return lax.dot_general(a, b, (((1,), (0,)), ((), ())), preferred_element_type=f32)


def mm_nt(a, b):
    return lax.dot_general(a, b, (((1,), (1,)), ((), ())), preferred_element_type=f32)


def mm_tn(a, b):
    return lax.dot_general(a, b, (((0,), (0,)), ((), ())), preferred_element_type=f32)


def low_lanes(shape):
    return lax.broadcasted_iota(jnp.int32, shape, len(shape) - 1) % 128 < HALF


def swap(value):
    return jnp.concatenate([value[:, HALF:], value[:, :HALF]], axis=1)


def part(q):
    return slice(q * 128, (q + 1) * 128)


def quarter(q):
    return pl.ds(q, 128, stride=QUAD)


def modes_of(received, to_modes):
    both = mm(to_modes, received)
    chosen = jnp.where(low_lanes((128, 128)), both[:128], both[128:])
    return (chosen + swap(chosen)).astype(bf16)


def rows_of(modes, to_rows):
    low = low_lanes((MX, 128))
    turned = swap(modes)
    stacked = jnp.concatenate(
        [
            jnp.where(low, modes, 0.0),
            jnp.where(low, 0.0, turned),
            jnp.where(low, turned, 0.0),
            jnp.where(low, 0.0, modes),
        ],
        axis=0,
    ).astype(bf16)
    return mm(to_rows, stacked).astype(bf16)


def own_block(shape):
    return (
        lax.broadcasted_iota(jnp.int32, shape, 0) % 8
        == lax.broadcasted_iota(jnp.int32, shape, 1) // HALF
    )


def gelu_slope(value):
    return 0.5 * (1.0 + lax.erf(value / math.sqrt(2.0))) + value * jnp.exp(
        -0.5 * value * value
    ) / math.sqrt(2.0 * math.pi)


def spectra_kernel(field_hbm, table_hbm, out_ref, field_ref, table_ref, woven_ref, sems):
    copies = [
        pltpu.make_async_copy(field_hbm, field_ref, sems.at[0]),
        pltpu.make_async_copy(table_hbm, table_ref, sems.at[1]),
    ]
    for copy in copies:
        copy.start()
    for copy in copies:
        copy.wait()
    table = table_ref[...]
    for q in range(QUAD):
        woven_ref[quarter(q), :] = mm_nt(table, field_ref[part(q), :])
    out_ref[...] = woven_ref[...].astype(bf16)


def copies_kernel(local_ref, out_ref):
    for block in range(BLOCKS):
        out_ref[block * 512 : (block + 1) * 512, :] = local_ref[...]


def modes_kernel(received_ref, to_modes_ref, modes_ref):
    modes_ref[...] = modes_of(received_ref[...], to_modes_ref[...])


def forward_modes_kernel(modes_ref, weight_ref, to_rows_ref, out_ref):
    wide = modes_ref[...].astype(f32)
    own = own_block((16, 512))
    sign = jnp.where(low_lanes((8, 128)), -1.0, 1.0)
    mixed = []
    for block in range(BLOCKS):
        mine = wide[block * 16 : (block + 1) * 16]
        spread = jnp.where(own, jnp.concatenate([mine] * 4, axis=1), 0.0).astype(bf16)
        product = mm(spread, weight_ref[block * 512 : (block + 1) * 512, :])
        mixed.append(product[:8] + sign * swap(product[8:]))
    out_ref[...] = rows_of(jnp.concatenate(mixed, axis=0), to_rows_ref[...])


def backward_modes_kernel(
    received_ref, weight_ref, modes_ref, to_modes_ref, to_rows_ref, pair_ref, out_ref
):
    grads = modes_of(received_ref[...], to_modes_ref[...])
    wide = grads.astype(f32)
    pair_ref[...] = jnp.where(
        low_lanes((128, 128)), modes_ref[...].astype(f32), wide
    ).astype(bf16)
    own = own_block((16, 512))
    low = low_lanes((8, 128))
    mixed = []
    for block in range(BLOCKS):
        real = wide[block * 16 : block * 16 + 8]
        imaginary = wide[block * 16 + 8 : block * 16 + 16]
        turned = jnp.concatenate(
            [jnp.where(low, real, imaginary), jnp.where(low, imaginary, -real)], axis=0
        ).astype(bf16)
        product = mm_nt(turned, weight_ref[block * 512 : (block + 1) * 512, :])
        product = jnp.where(own, product, 0.0)
        folded = product[:, :128] + product[:, 128:256] + product[:, 256:384] + product[:, 384:]
        folded = folded + swap(folded)
        mixed.append(jnp.where(low, folded[:8], folded[8:]))
    out_ref[...] = rows_of(jnp.concatenate(mixed, axis=0), to_rows_ref[...])


def linear_kernel(field_ref, cotangent_hbm, point_ref, bias_ref, out_ref, cotangent_ref, sems):
    copy = pltpu.make_async_copy(cotangent_hbm, cotangent_ref, sems.at[0])
    copy.start()
    for q in range(QUAD):
        out_ref[part(q), :] = mm(point_ref[...], field_ref[part(q), :]) + bias_ref[...]
    copy.wait()


def slope_kernel(
    received_ref, linear_ref, cotangent_ref, inverse_ref, grad_ref, out_ref, woven_ref
):
    inverse = inverse_ref[...]
    woven_ref[...] = received_ref[...].astype(f32)
    rows = [woven_ref[quarter(q), :].astype(bf16) for q in range(QUAD)]
    for q in range(QUAD):
        value = mm_tn(rows[q], inverse) + linear_ref[part(q), :]
        grad = (cotangent_ref[part(q), :].astype(f32) * gelu_slope(value)).astype(bf16)
        grad_ref[part(q), :] = grad
        woven_ref[quarter(q), :] = mm_nt(inverse, grad)
    out_ref[...] = woven_ref[...].astype(bf16)


def field_kernel(
    received_ref,
    grad_ref,
    point_ref,
    forward_ref,
    weight_hbm,
    first_hbm,
    second_hbm,
    out_hbm,
    weight_out,
    first_out,
    second_out,
    out_ref,
    woven_ref,
    sems,
):
    loads = []
    for n, (source, target) in enumerate(
        ((weight_hbm, weight_out), (first_hbm, first_out), (second_hbm, second_out))
    ):
        copy = pltpu.make_async_copy(source, target, sems.at[QUAD + n])
        copy.start()
        loads.append(copy)
    forward = forward_ref[...]
    woven_ref[...] = received_ref[...].astype(f32)
    copies = []
    for q in range(QUAD):
        rows = woven_ref[quarter(q), :].astype(bf16)
        value = mm_tn(rows, forward) + mm(point_ref[...], grad_ref[part(q), :])
        out_ref[part(q), :] = value.astype(bf16)
        copy = pltpu.make_async_copy(out_ref.at[part(q)], out_hbm.at[part(q)], sems.at[q])
        copy.start()
        copies.append(copy)
    for copy in loads + copies:
        copy.wait()


def adam_kernel(
    pair_ref,
    pick_ref,
    weight_ref,
    first_ref,
    second_ref,
    new_weight_hbm,
    new_first_hbm,
    new_second_hbm,
    made_ref,
    sems,
):
    bias_one = 1.0 - beta_one**adam_step
    bias_two = 1.0 - beta_two**adam_step
    wide = pair_ref[...].astype(f32)
    turned = []
    for sample in range(8):
        turned.append(-wide[sample * 16 + 8 : sample * 16 + 16])
        turned.append(wide[sample * 16 : sample * 16 + 8])
    both = jnp.concatenate([wide, jnp.concatenate(turned, axis=0)], axis=1).astype(bf16)
    left = mm(both, pick_ref[...])
    left = jnp.concatenate([left, swap(left)], axis=0).astype(bf16)
    low = low_lanes((128, 128))
    right = jnp.concatenate([jnp.where(low, swap(wide), 0.0), jnp.where(low, 0.0, wide)], axis=0)
    mode = lax.broadcasted_iota(jnp.int32, (256, 128), 0) % 8
    spread = [jnp.where(mode == j, right, 0.0).astype(bf16) for j in range(8)]
    gradients = mm_tn(left, jnp.concatenate(spread, axis=1))
    copies = []
    for j in range(8):
        at = slice(j * 64, (j + 1) * 64)
        gradient = gradients[:64, j * 128 : (j + 1) * 128]
        first = beta_one * first_ref[at, :] + (1.0 - beta_one) * gradient
        second = beta_two * second_ref[at, :] + (1.0 - beta_two) * gradient * gradient
        step = learn_rate * (first / bias_one) / (jnp.sqrt(second / bias_two) + epsilon_adam)
        made_ref[0, at, :] = weight_ref[at, :] - step
        made_ref[1, at, :] = first
        made_ref[2, at, :] = second
        if j % 2 == 1:
            at = slice((j - 1) * 64, (j + 1) * 64)
            for n, target in enumerate((new_weight_hbm, new_first_hbm, new_second_hbm)):
                copy = pltpu.make_async_copy(
                    made_ref.at[n, at], target.at[at], sems.at[3 * (j // 2) + n]
                )
                copy.start()
                copies.append(copy)
    for copy in copies:
        copy.wait()


HBM = pl.BlockSpec(memory_space=pltpu.HBM)
VMEM = pl.BlockSpec(memory_space=pltpu.VMEM)


def call(kernel, outs, *arrays, scratch=(), far=(), far_out=(), near_out=False):
    arrays = [
        pltpu.with_memory_space_constraint(a, pltpu.HBM) if n in far else a
        for n, a in enumerate(arrays)
    ]
    place = pltpu.VMEM if near_out else jax.ShapeDtypeStruct
    return pl.pallas_call(
        kernel,
        out_shape=[place(shape, dtype) for shape, dtype in outs],
        in_specs=[HBM if n in far else VMEM for n in range(len(arrays))],
        out_specs=[HBM if n in far_out else VMEM for n in range(len(outs))],
        scratch_shapes=list(scratch),
        compiler_params=pltpu.CompilerParams(vmem_limit_bytes=24 * 1024 * 1024),
    )(*arrays)


def exchange(array, axis):
    groups = [GRID_ORDER if axis == "grid" else DP_ORDER]
    return lax.all_to_all(
        array, axis, split_axis=0, concat_axis=0, axis_index_groups=groups, tiled=True
    )


def shards(
    in_field, out_grad, point_weight, point_bias, spectral_weight, first_moment, second_moment
):
    forward, inverse, to_modes, to_rows, pick = (jnp.asarray(t) for t in tables())
    field = in_field.reshape(SLAB * C, NY)
    cotangent = out_grad.reshape(SLAB * C, NY)
    zero = jnp.zeros_like(point_weight)
    point = jnp.block([[point_weight, zero], [zero, point_weight]])
    bias = jnp.concatenate([point_bias, point_bias]).reshape(128, 1)
    message = [((512, 128), bf16)]

    plane = pltpu.VMEM((512, 512), bf16)
    woven = pltpu.VMEM((512, 128), f32)
    dma = pltpu.SemaphoreType.DMA

    (sent,) = call(
        spectra_kernel,
        message,
        field,
        forward,
        far=(0, 1),
        scratch=(plane, pltpu.VMEM((128, 512), bf16), woven, dma((2,))),
    )
    columns = exchange(sent, "grid")

    local = spectral_weight.astype(bf16).reshape(8, 2, C, C).transpose(0, 2, 1, 3).reshape(512, 128)
    (copies,) = call(copies_kernel, [((BLOCKS * 512, 128), bf16)], local, near_out=True)
    whole = exchange(copies, "dp")

    (modes,) = call(modes_kernel, [((128, 128), bf16)], columns, to_modes)
    linear, near = call(
        linear_kernel,
        [((512, 512), f32), ((512, 512), bf16)],
        field,
        cotangent,
        point.T,
        bias,
        far=(1,),
        scratch=(dma((1,)),),
        near_out=True,
    )
    modes, linear, near = lax.optimization_barrier((modes, linear, near))
    (sent,) = call(forward_modes_kernel, message, modes, whole, to_rows)
    received = exchange(sent, "grid")
    pre_grad, sent = call(
        slope_kernel,
        [((512, 512), bf16)] + message,
        received,
        linear,
        near,
        inverse,
        scratch=(woven,),
    )
    columns = exchange(sent, "grid")
    pair, sent = call(
        backward_modes_kernel,
        [((128, 128), bf16)] + message,
        columns,
        whole,
        modes,
        to_modes,
        to_rows,
    )
    received, pair = lax.optimization_barrier((exchange(sent, "grid"), pair))
    pair = exchange(pair, "dp")
    masters = [
        m.reshape(8, 2, C // 2, 128).transpose(0, 2, 1, 3).reshape(512, 128)
        for m in (spectral_weight, first_moment, second_moment)
    ]
    flat = [((512, 128), f32)] * 3
    grad_field, *near = call(
        field_kernel,
        [((512, 512), bf16)] + flat,
        received,
        pre_grad,
        point,
        forward,
        *masters,
        far=(4, 5, 6),
        far_out=(0,),
        scratch=(plane, woven, dma((QUAD + 3,))),
    )
    made = call(
        adam_kernel,
        flat,
        pair,
        pick,
        *near,
        far_out=(0, 1, 2),
        scratch=(pltpu.VMEM((3, 512, 128), f32), dma((12,))),
    )
    new_weight, new_first, new_second = (
        m.reshape(8, C // 2, 2, 128).transpose(0, 2, 1, 3).reshape(spectral_weight.shape)
        for m in made
    )
    return (grad_field.reshape(in_field.shape), new_weight, new_first, new_second)


def solution(mesh):
    split = P("dp", "grid", None, None)
    return jax.shard_map(
        shards,
        mesh=mesh,
        in_specs=(split, split, P(), P(), split, split, split),
        out_specs=(split, split, split, split),
        check_vma=False,
    )
```

```python
import math

import jax
import jax.numpy as jnp
import numpy as np
from jax import lax
from jax.experimental import pallas as pl
from jax.experimental.pallas import tpu as pltpu
from jax.sharding import PartitionSpec as P

C = 64
NX = 512
NY = 512
MX = 64
MY = 64
SLAB = 8
QUAD = 4
HALF = 64
BLOCKS = 8

GRID_ORDER = [(20 + 45 * k) % 64 for k in range(64)]
DP_ORDER = [(5 + 3 * k) % 8 for k in range(8)]

beta_one = 0.9
beta_two = 0.999
learn_rate = 0.01
adam_step = 100
epsilon_adam = 1e-08

f32 = jnp.float32
bf16 = jnp.bfloat16


def tables():
    frequency = np.array(GRID_ORDER)
    position = np.arange(NY)
    angles = ((position[:, None] * frequency[None, :]) % NY).astype(np.float32) * np.float32(
        2.0 * math.pi / NY
    )
    cos, sin = np.cos(angles), np.sin(angles)
    forward = np.stack([cos, -sin], axis=-1).reshape(NY, 2 * MY).T
    factor = np.where(frequency == 0, 1.0, 2.0).astype(np.float32) / np.float32(NX * NY)
    inverse = np.stack([factor * cos, -factor * sin], axis=-1).reshape(NY, 2 * MY).T

    column = np.arange(MX)
    wavenumber = np.where(column < MX // 2, column, NX - MX + column)
    rows = np.arange(NX)
    turn = ((wavenumber[:, None] * rows[None, :]) % NX).astype(np.float32) * np.float32(
        2.0 * math.pi / NX
    )
    by_order = lambda t: (
        t.reshape(BLOCKS, 8, NX // SLAB, SLAB)[DP_ORDER][:, :, GRID_ORDER].reshape(MX, NX)
    )
    col_cos, col_sin = by_order(np.cos(turn)), by_order(np.sin(turn))

    by_slab = lambda t: t.reshape(BLOCKS, 8, NX // SLAB, QUAD, 2)
    c, s = by_slab(col_cos), by_slab(col_sin)
    to_modes = np.stack([np.stack([c, s], 0), np.stack([-s, c], 0)], 0)
    to_modes = to_modes.transpose(6, 2, 0, 3, 4, 1, 5).reshape(256, 512)

    by_slab = lambda t: t.reshape(MX, NX // SLAB, QUAD, 2)
    c, s = by_slab(col_cos), by_slab(col_sin)
    to_rows = np.stack([np.stack([c, -s], 0), np.stack([s, c], 0)], 0)
    to_rows = to_rows.transpose(3, 0, 4, 1, 5, 2).reshape(512, 256)

    pick = np.zeros((2, 128, 2, C // 2, 2), np.float32)
    for c in range(C):
        for p in range(2):
            pick[p, c, c % 2, c // 2, p] = 1.0
    pick = pick.reshape(256, 128)
    made = (forward, inverse, to_modes, to_rows, pick)
    return tuple(np.asarray(t, np.float32).astype(jnp.bfloat16) for t in made)


def mm(a, b):
    return lax.dot_general(a, b, (((1,), (0,)), ((), ())), preferred_element_type=f32)


def mm_nt(a, b):
    return lax.dot_general(a, b, (((1,), (1,)), ((), ())), preferred_element_type=f32)


def mm_tn(a, b):
    return lax.dot_general(a, b, (((0,), (0,)), ((), ())), preferred_element_type=f32)


def low_lanes(shape):
    return lax.broadcasted_iota(jnp.int32, shape, len(shape) - 1) % 128 < HALF


def swap(value):
    return jnp.concatenate([value[:, HALF:], value[:, :HALF]], axis=1)


def part(q):
    return slice(q * 128, (q + 1) * 128)


def quarter(q):
    return pl.ds(q, 128, stride=QUAD)


def modes_of(received, to_modes):
    both = mm(to_modes, received)
    chosen = jnp.where(low_lanes((128, 128)), both[:128], both[128:])
    return (chosen + swap(chosen)).astype(bf16)


def rows_of(modes, to_rows):
    low = low_lanes((MX, 128))
    turned = swap(modes)
    stacked = jnp.concatenate(
        [
            jnp.where(low, modes, 0.0),
            jnp.where(low, 0.0, turned),
            jnp.where(low, turned, 0.0),
            jnp.where(low, 0.0, modes),
        ],
        axis=0,
    ).astype(bf16)
    return mm(to_rows, stacked).astype(bf16)


def own_block(shape):
    return (
        lax.broadcasted_iota(jnp.int32, shape, 0) % 8
        == lax.broadcasted_iota(jnp.int32, shape, 1) // HALF
    )


def gelu_slope(value):
    return 0.5 * (1.0 + lax.erf(value / math.sqrt(2.0))) + value * jnp.exp(
        -0.5 * value * value
    ) / math.sqrt(2.0 * math.pi)


def spectra_kernel(field_hbm, table_hbm, out_ref, field_ref, table_ref, woven_ref, sems):
    copies = [
        pltpu.make_async_copy(field_hbm, field_ref, sems.at[0]),
        pltpu.make_async_copy(table_hbm, table_ref, sems.at[1]),
    ]
    for copy in copies:
        copy.start()
    for copy in copies:
        copy.wait()
    table = table_ref[...]
    for q in range(QUAD):
        woven_ref[quarter(q), :] = mm_nt(table, field_ref[part(q), :])
    out_ref[...] = woven_ref[...].astype(bf16)


def copies_kernel(local_ref, out_ref):
    for block in range(BLOCKS):
        out_ref[block * 512 : (block + 1) * 512, :] = local_ref[...]


def modes_kernel(received_ref, to_modes_ref, modes_ref):
    modes_ref[...] = modes_of(received_ref[...], to_modes_ref[...])


def forward_modes_kernel(modes_ref, weight_ref, to_rows_ref, out_ref):
    wide = modes_ref[...].astype(f32)
    own = own_block((16, 512))
    sign = jnp.where(low_lanes((8, 128)), -1.0, 1.0)
    mixed = []
    for block in range(BLOCKS):
        mine = wide[block * 16 : (block + 1) * 16]
        spread = jnp.where(own, jnp.concatenate([mine] * 4, axis=1), 0.0).astype(bf16)
        product = mm(spread, weight_ref[block * 512 : (block + 1) * 512, :])
        mixed.append(product[:8] + sign * swap(product[8:]))
    out_ref[...] = rows_of(jnp.concatenate(mixed, axis=0), to_rows_ref[...])


def backward_modes_kernel(
    received_ref, weight_ref, modes_ref, to_modes_ref, to_rows_ref, pair_ref, out_ref
):
    grads = modes_of(received_ref[...], to_modes_ref[...])
    wide = grads.astype(f32)
    pair_ref[...] = jnp.where(
        low_lanes((128, 128)), modes_ref[...].astype(f32), wide
    ).astype(bf16)
    own = own_block((16, 512))
    low = low_lanes((8, 128))
    mixed = []
    for block in range(BLOCKS):
        real = wide[block * 16 : block * 16 + 8]
        imaginary = wide[block * 16 + 8 : block * 16 + 16]
        turned = jnp.concatenate(
            [jnp.where(low, real, imaginary), jnp.where(low, imaginary, -real)], axis=0
        ).astype(bf16)
        product = mm_nt(turned, weight_ref[block * 512 : (block + 1) * 512, :])
        product = jnp.where(own, product, 0.0)
        folded = product[:, :128] + product[:, 128:256] + product[:, 256:384] + product[:, 384:]
        folded = folded + swap(folded)
        mixed.append(jnp.where(low, folded[:8], folded[8:]))
    out_ref[...] = rows_of(jnp.concatenate(mixed, axis=0), to_rows_ref[...])


def linear_kernel(field_ref, cotangent_hbm, point_ref, bias_ref, out_ref, cotangent_ref, sems):
    copy = pltpu.make_async_copy(cotangent_hbm, cotangent_ref, sems.at[0])
    copy.start()
    for q in range(QUAD):
        out_ref[part(q), :] = mm(point_ref[...], field_ref[part(q), :]) + bias_ref[...]
    copy.wait()


def slope_kernel(
    received_ref, linear_ref, cotangent_ref, inverse_ref, grad_ref, out_ref, woven_ref
):
    inverse = inverse_ref[...]
    woven_ref[...] = received_ref[...].astype(f32)
    rows = [woven_ref[quarter(q), :].astype(bf16) for q in range(QUAD)]
    for q in range(QUAD):
        value = mm_tn(rows[q], inverse) + linear_ref[part(q), :]
        grad = (cotangent_ref[part(q), :].astype(f32) * gelu_slope(value)).astype(bf16)
        grad_ref[part(q), :] = grad
        woven_ref[quarter(q), :] = mm_nt(inverse, grad)
    out_ref[...] = woven_ref[...].astype(bf16)


def field_kernel(
    received_ref,
    grad_ref,
    point_ref,
    forward_ref,
    weight_hbm,
    first_hbm,
    second_hbm,
    out_hbm,
    weight_out,
    first_out,
    second_out,
    out_ref,
    woven_ref,
    sems,
):
    loads = []
    for n, (source, target) in enumerate(
        ((weight_hbm, weight_out), (first_hbm, first_out), (second_hbm, second_out))
    ):
        copy = pltpu.make_async_copy(source, target, sems.at[QUAD + n])
        copy.start()
        loads.append(copy)
    forward = forward_ref[...]
    woven_ref[...] = received_ref[...].astype(f32)
    copies = []
    for q in range(QUAD):
        rows = woven_ref[quarter(q), :].astype(bf16)
        value = mm_tn(rows, forward) + mm(point_ref[...], grad_ref[part(q), :])
        out_ref[part(q), :] = value.astype(bf16)
        copy = pltpu.make_async_copy(out_ref.at[part(q)], out_hbm.at[part(q)], sems.at[q])
        copy.start()
        copies.append(copy)
    for copy in loads + copies:
        copy.wait()


def adam_kernel(
    pair_ref,
    pick_ref,
    weight_ref,
    first_ref,
    second_ref,
    new_weight_hbm,
    new_first_hbm,
    new_second_hbm,
    made_ref,
    sems,
):
    bias_one = 1.0 - beta_one**adam_step
    bias_two = 1.0 - beta_two**adam_step
    wide = pair_ref[...].astype(f32)
    turned = []
    for sample in range(8):
        turned.append(-wide[sample * 16 + 8 : sample * 16 + 16])
        turned.append(wide[sample * 16 : sample * 16 + 8])
    both = jnp.concatenate([wide, jnp.concatenate(turned, axis=0)], axis=1).astype(bf16)
    left = mm(both, pick_ref[...])
    left = jnp.concatenate([left, swap(left)], axis=0).astype(bf16)
    low = low_lanes((128, 128))
    right = jnp.concatenate([jnp.where(low, swap(wide), 0.0), jnp.where(low, 0.0, wide)], axis=0)
    mode = lax.broadcasted_iota(jnp.int32, (256, 128), 0) % 8
    spread = [jnp.where(mode == j, right, 0.0).astype(bf16) for j in range(8)]
    gradients = mm_tn(left, jnp.concatenate(spread, axis=1))
    copies = []
    for j in range(8):
        at = slice(j * 64, (j + 1) * 64)
        gradient = gradients[:64, j * 128 : (j + 1) * 128]
        first = beta_one * first_ref[at, :] + (1.0 - beta_one) * gradient
        second = beta_two * second_ref[at, :] + (1.0 - beta_two) * gradient * gradient
        step = learn_rate * (first / bias_one) / (jnp.sqrt(second / bias_two) + epsilon_adam)
        made_ref[0, at, :] = weight_ref[at, :] - step
        made_ref[1, at, :] = first
        made_ref[2, at, :] = second
        if j % 2 == 1:
            at = slice((j - 1) * 64, (j + 1) * 64)
            for n, target in enumerate((new_weight_hbm, new_first_hbm, new_second_hbm)):
                copy = pltpu.make_async_copy(
                    made_ref.at[n, at], target.at[at], sems.at[3 * (j // 2) + n]
                )
                copy.start()
                copies.append(copy)
    for copy in copies:
        copy.wait()


HBM = pl.BlockSpec(memory_space=pltpu.HBM)
VMEM = pl.BlockSpec(memory_space=pltpu.VMEM)


def call(kernel, outs, *arrays, scratch=(), far=(), far_out=(), near_out=False):
    arrays = [
        pltpu.with_memory_space_constraint(a, pltpu.HBM) if n in far else a
        for n, a in enumerate(arrays)
    ]
    place = pltpu.VMEM if near_out else jax.ShapeDtypeStruct
    return pl.pallas_call(
        kernel,
        out_shape=[place(shape, dtype) for shape, dtype in outs],
        in_specs=[HBM if n in far else VMEM for n in range(len(arrays))],
        out_specs=[HBM if n in far_out else VMEM for n in range(len(outs))],
        scratch_shapes=list(scratch),
        compiler_params=pltpu.CompilerParams(vmem_limit_bytes=24 * 1024 * 1024),
    )(*arrays)


def exchange(array, axis):
    groups = [GRID_ORDER if axis == "grid" else DP_ORDER]
    return lax.all_to_all(
        array, axis, split_axis=0, concat_axis=0, axis_index_groups=groups, tiled=True
    )


def shards(
    in_field, out_grad, point_weight, point_bias, spectral_weight, first_moment, second_moment
):
    forward, inverse, to_modes, to_rows, pick = (jnp.asarray(t) for t in tables())
    field = in_field.reshape(SLAB * C, NY)
    cotangent = out_grad.reshape(SLAB * C, NY)
    zero = jnp.zeros_like(point_weight)
    point = jnp.block([[point_weight, zero], [zero, point_weight]])
    bias = jnp.concatenate([point_bias, point_bias]).reshape(128, 1)
    message = [((512, 128), bf16)]

    plane = pltpu.VMEM((512, 512), bf16)
    woven = pltpu.VMEM((512, 128), f32)
    dma = pltpu.SemaphoreType.DMA

    (sent,) = call(
        spectra_kernel,
        message,
        field,
        forward,
        far=(0, 1),
        scratch=(plane, pltpu.VMEM((128, 512), bf16), woven, dma((2,))),
    )
    columns = exchange(sent, "grid")

    local = spectral_weight.astype(bf16).reshape(8, 2, C, C).transpose(0, 2, 1, 3).reshape(512, 128)
    (copies,) = call(copies_kernel, [((BLOCKS * 512, 128), bf16)], local, near_out=True)
    whole = exchange(copies, "dp")

    (modes,) = call(modes_kernel, [((128, 128), bf16)], columns, to_modes)
    linear, near = call(
        linear_kernel,
        [((512, 512), f32), ((512, 512), bf16)],
        field,
        cotangent,
        point.T,
        bias,
        far=(1,),
        scratch=(dma((1,)),),
        near_out=True,
    )
    modes, linear, near = lax.optimization_barrier((modes, linear, near))
    (sent,) = call(forward_modes_kernel, message, modes, whole, to_rows)
    received = exchange(sent, "grid")
    pre_grad, sent = call(
        slope_kernel,
        [((512, 512), bf16)] + message,
        received,
        linear,
        near,
        inverse,
        scratch=(woven,),
    )
    columns = exchange(sent, "grid")
    pair, sent = call(
        backward_modes_kernel,
        [((128, 128), bf16)] + message,
        columns,
        whole,
        modes,
        to_modes,
        to_rows,
    )
    received, pair = lax.optimization_barrier((exchange(sent, "grid"), pair))
    pair = exchange(pair, "dp")
    masters = [
        m.reshape(8, 2, C // 2, 128).transpose(0, 2, 1, 3).reshape(512, 128)
        for m in (spectral_weight, first_moment, second_moment)
    ]
    flat = [((512, 128), f32)] * 3
    grad_field, *near = call(
        field_kernel,
        [((512, 512), bf16)] + flat,
        received,
        pre_grad,
        point,
        forward,
        *masters,
        far=(4, 5, 6),
        far_out=(0,),
        scratch=(plane, woven, dma((QUAD + 3,))),
    )
    made = call(
        adam_kernel,
        flat,
        pair,
        pick,
        *near,
        far_out=(0, 1, 2),
        scratch=(pltpu.VMEM((3, 512, 128), f32), dma((12,))),
    )
    new_weight, new_first, new_second = (
        m.reshape(8, C // 2, 2, 128).transpose(0, 2, 1, 3).reshape(spectral_weight.shape)
        for m in made
    )
    return (grad_field.reshape(in_field.shape), new_weight, new_first, new_second)


def solution(mesh):
    split = P("dp", "grid", None, None)
    return jax.shard_map(
        shards,
        mesh=mesh,
        in_specs=(split, split, P(), P(), split, split, split),
        out_specs=(split, split, split, split),
        check_vma=False,
    )
```

```python
import math

import jax
import jax.numpy as jnp
import numpy as np
from jax import lax
from jax.experimental import pallas as pl
from jax.experimental.pallas import tpu as pltpu
from jax.sharding import PartitionSpec as P

C = 64
NX = 512
NY = 512
MX = 64
MY = 64
SLAB = 8
QUAD = 4
HALF = 64
BLOCKS = 8

GRID_ORDER = [(20 + 45 * k) % 64 for k in range(64)]
DP_ORDER = [(5 + 3 * k) % 8 for k in range(8)]

beta_one = 0.9
beta_two = 0.999
learn_rate = 0.01
adam_step = 100
epsilon_adam = 1e-08

f32 = jnp.float32
bf16 = jnp.bfloat16


def tables():
    frequency = np.array(GRID_ORDER)
    position = np.arange(NY)
    angles = ((position[:, None] * frequency[None, :]) % NY).astype(np.float32) * np.float32(
        2.0 * math.pi / NY
    )
    cos, sin = np.cos(angles), np.sin(angles)
    forward = np.stack([cos, -sin], axis=-1).reshape(NY, 2 * MY).T
    factor = np.where(frequency == 0, 1.0, 2.0).astype(np.float32) / np.float32(NX * NY)
    inverse = np.stack([factor * cos, -factor * sin], axis=-1).reshape(NY, 2 * MY).T

    column = np.arange(MX)
    wavenumber = np.where(column < MX // 2, column, NX - MX + column)
    rows = np.arange(NX)
    turn = ((wavenumber[:, None] * rows[None, :]) % NX).astype(np.float32) * np.float32(
        2.0 * math.pi / NX
    )
    by_order = lambda t: (
        t.reshape(BLOCKS, 8, NX // SLAB, SLAB)[DP_ORDER][:, :, GRID_ORDER].reshape(MX, NX)
    )
    col_cos, col_sin = by_order(np.cos(turn)), by_order(np.sin(turn))

    by_slab = lambda t: t.reshape(BLOCKS, 8, NX // SLAB, QUAD, 2)
    c, s = by_slab(col_cos), by_slab(col_sin)
    to_modes = np.stack([np.stack([c, s], 0), np.stack([-s, c], 0)], 0)
    to_modes = to_modes.transpose(6, 2, 0, 3, 4, 1, 5).reshape(256, 512)

    by_slab = lambda t: t.reshape(MX, NX // SLAB, QUAD, 2)
    c, s = by_slab(col_cos), by_slab(col_sin)
    to_rows = np.stack([np.stack([c, -s], 0), np.stack([s, c], 0)], 0)
    to_rows = to_rows.transpose(3, 0, 4, 1, 5, 2).reshape(512, 256)

    pick = np.zeros((2, 128, 2, C // 2, 2), np.float32)
    for c in range(C):
        for p in range(2):
            pick[p, c, c % 2, c // 2, p] = 1.0
    pick = pick.reshape(256, 128)
    made = (forward, inverse, to_modes, to_rows, pick)
    return tuple(np.asarray(t, np.float32).astype(jnp.bfloat16) for t in made)


def mm(a, b):
    return lax.dot_general(a, b, (((1,), (0,)), ((), ())), preferred_element_type=f32)


def mm_nt(a, b):
    return lax.dot_general(a, b, (((1,), (1,)), ((), ())), preferred_element_type=f32)


def mm_tn(a, b):
    return lax.dot_general(a, b, (((0,), (0,)), ((), ())), preferred_element_type=f32)


def low_lanes(shape):
    return lax.broadcasted_iota(jnp.int32, shape, len(shape) - 1) % 128 < HALF


def swap(value):
    return jnp.concatenate([value[:, HALF:], value[:, :HALF]], axis=1)


def part(q):
    return slice(q * 128, (q + 1) * 128)


def quarter(q):
    return pl.ds(q, 128, stride=QUAD)


def modes_of(received, to_modes):
    both = mm(to_modes, received)
    chosen = jnp.where(low_lanes((128, 128)), both[:128], both[128:])
    return (chosen + swap(chosen)).astype(bf16)


def rows_of(modes, to_rows):
    low = low_lanes((MX, 128))
    turned = swap(modes)
    stacked = jnp.concatenate(
        [
            jnp.where(low, modes, 0.0),
            jnp.where(low, 0.0, turned),
            jnp.where(low, turned, 0.0),
            jnp.where(low, 0.0, modes),
        ],
        axis=0,
    ).astype(bf16)
    return mm(to_rows, stacked).astype(bf16)


def own_block(shape):
    return (
        lax.broadcasted_iota(jnp.int32, shape, 0) % 8
        == lax.broadcasted_iota(jnp.int32, shape, 1) // HALF
    )


def gelu_slope(value):
    return 0.5 * (1.0 + lax.erf(value / math.sqrt(2.0))) + value * jnp.exp(
        -0.5 * value * value
    ) / math.sqrt(2.0 * math.pi)


def spectra_kernel(field_hbm, table_hbm, out_ref, field_ref, table_ref, woven_ref, sems):
    copies = [
        pltpu.make_async_copy(field_hbm, field_ref, sems.at[0]),
        pltpu.make_async_copy(table_hbm, table_ref, sems.at[1]),
    ]
    for copy in copies:
        copy.start()
    for copy in copies:
        copy.wait()
    table = table_ref[...]
    for q in range(QUAD):
        woven_ref[quarter(q), :] = mm_nt(table, field_ref[part(q), :])
    out_ref[...] = woven_ref[...].astype(bf16)


def copies_kernel(local_ref, out_ref):
    for block in range(BLOCKS):
        out_ref[block * 512 : (block + 1) * 512, :] = local_ref[...]


def modes_kernel(received_ref, to_modes_ref, modes_ref):
    modes_ref[...] = modes_of(received_ref[...], to_modes_ref[...])


def forward_modes_kernel(modes_ref, weight_ref, to_rows_ref, out_ref):
    wide = modes_ref[...].astype(f32)
    own = own_block((16, 512))
    sign = jnp.where(low_lanes((8, 128)), -1.0, 1.0)
    mixed = []
    for block in range(BLOCKS):
        mine = wide[block * 16 : (block + 1) * 16]
        spread = jnp.where(own, jnp.concatenate([mine] * 4, axis=1), 0.0).astype(bf16)
        product = mm(spread, weight_ref[block * 512 : (block + 1) * 512, :])
        mixed.append(product[:8] + sign * swap(product[8:]))
    out_ref[...] = rows_of(jnp.concatenate(mixed, axis=0), to_rows_ref[...])


def backward_modes_kernel(
    received_ref, weight_ref, modes_ref, to_modes_ref, to_rows_ref, pair_ref, out_ref
):
    grads = modes_of(received_ref[...], to_modes_ref[...])
    wide = grads.astype(f32)
    pair_ref[...] = jnp.where(
        low_lanes((128, 128)), modes_ref[...].astype(f32), wide
    ).astype(bf16)
    own = own_block((16, 512))
    low = low_lanes((8, 128))
    mixed = []
    for block in range(BLOCKS):
        real = wide[block * 16 : block * 16 + 8]
        imaginary = wide[block * 16 + 8 : block * 16 + 16]
        turned = jnp.concatenate(
            [jnp.where(low, real, imaginary), jnp.where(low, imaginary, -real)], axis=0
        ).astype(bf16)
        product = mm_nt(turned, weight_ref[block * 512 : (block + 1) * 512, :])
        product = jnp.where(own, product, 0.0)
        folded = product[:, :128] + product[:, 128:256] + product[:, 256:384] + product[:, 384:]
        folded = folded + swap(folded)
        mixed.append(jnp.where(low, folded[:8], folded[8:]))
    out_ref[...] = rows_of(jnp.concatenate(mixed, axis=0), to_rows_ref[...])


def linear_kernel(field_ref, cotangent_hbm, point_ref, bias_ref, out_ref, cotangent_ref, sems):
    copy = pltpu.make_async_copy(cotangent_hbm, cotangent_ref, sems.at[0])
    copy.start()
    for q in range(QUAD):
        out_ref[part(q), :] = mm(point_ref[...], field_ref[part(q), :]) + bias_ref[...]
    copy.wait()


def slope_kernel(
    received_ref, linear_ref, cotangent_ref, inverse_ref, grad_ref, out_ref, woven_ref
):
    inverse = inverse_ref[...]
    woven_ref[...] = received_ref[...].astype(f32)
    rows = [woven_ref[quarter(q), :].astype(bf16) for q in range(QUAD)]
    for q in range(QUAD):
        value = mm_tn(rows[q], inverse) + linear_ref[part(q), :]
        grad = (cotangent_ref[part(q), :].astype(f32) * gelu_slope(value)).astype(bf16)
        grad_ref[part(q), :] = grad
        woven_ref[quarter(q), :] = mm_nt(inverse, grad)
    out_ref[...] = woven_ref[...].astype(bf16)


def field_kernel(
    received_ref,
    grad_ref,
    point_ref,
    forward_ref,
    weight_hbm,
    first_hbm,
    second_hbm,
    out_hbm,
    weight_out,
    first_out,
    second_out,
    out_ref,
    woven_ref,
    sems,
):
    loads = []
    for n, (source, target) in enumerate(
        ((weight_hbm, weight_out), (first_hbm, first_out), (second_hbm, second_out))
    ):
        copy = pltpu.make_async_copy(source, target, sems.at[QUAD + n])
        copy.start()
        loads.append(copy)
    forward = forward_ref[...]
    woven_ref[...] = received_ref[...].astype(f32)
    copies = []
    for q in range(QUAD):
        rows = woven_ref[quarter(q), :].astype(bf16)
        value = mm_tn(rows, forward) + mm(point_ref[...], grad_ref[part(q), :])
        out_ref[part(q), :] = value.astype(bf16)
        copy = pltpu.make_async_copy(out_ref.at[part(q)], out_hbm.at[part(q)], sems.at[q])
        copy.start()
        copies.append(copy)
    for copy in loads:
        copy.wait()
    return copies


def adam_kernel(
    pair_ref,
    pick_ref,
    weight_ref,
    first_ref,
    second_ref,
    new_weight_hbm,
    new_first_hbm,
    new_second_hbm,
    made_ref,
    sems,
):
    bias_one = 1.0 - beta_one**adam_step
    bias_two = 1.0 - beta_two**adam_step
    wide = pair_ref[...].astype(f32)
    turned = []
    for sample in range(8):
        turned.append(-wide[sample * 16 + 8 : sample * 16 + 16])
        turned.append(wide[sample * 16 : sample * 16 + 8])
    both = jnp.concatenate([wide, jnp.concatenate(turned, axis=0)], axis=1).astype(bf16)
    left = mm(both, pick_ref[...])
    left = jnp.concatenate([left, swap(left)], axis=0).astype(bf16)
    low = low_lanes((128, 128))
    right = jnp.concatenate([jnp.where(low, swap(wide), 0.0), jnp.where(low, 0.0, wide)], axis=0)
    mode = lax.broadcasted_iota(jnp.int32, (256, 128), 0) % 8
    spread = [jnp.where(mode == j, right, 0.0).astype(bf16) for j in range(8)]
    gradients = mm_tn(left, jnp.concatenate(spread, axis=1))
    copies = []
    for j in range(8):
        at = slice(j * 64, (j + 1) * 64)
        gradient = gradients[:64, j * 128 : (j + 1) * 128]
        first = beta_one * first_ref[at, :] + (1.0 - beta_one) * gradient
        second = beta_two * second_ref[at, :] + (1.0 - beta_two) * gradient * gradient
        step = learn_rate * (first / bias_one) / (jnp.sqrt(second / bias_two) + epsilon_adam)
        made_ref[0, at, :] = weight_ref[at, :] - step
        made_ref[1, at, :] = first
        made_ref[2, at, :] = second
        if j % 2 == 1:
            at = slice((j - 1) * 64, (j + 1) * 64)
            for n, target in enumerate((new_weight_hbm, new_first_hbm, new_second_hbm)):
                copy = pltpu.make_async_copy(
                    made_ref.at[n, at], target.at[at], sems.at[3 * (j // 2) + n]
                )
                copy.start()
                copies.append(copy)
    for copy in copies:
        copy.wait()


def last_kernel(
    received_ref,
    grad_ref,
    point_ref,
    forward_ref,
    weight_hbm,
    first_hbm,
    second_hbm,
    pair_ref,
    pick_ref,
    out_hbm,
    new_weight_hbm,
    new_first_hbm,
    new_second_hbm,
    weight_ref,
    first_ref,
    second_ref,
    out_ref,
    woven_ref,
    made_ref,
    sems,
    made_sems,
):
    copies = field_kernel(
        received_ref,
        grad_ref,
        point_ref,
        forward_ref,
        weight_hbm,
        first_hbm,
        second_hbm,
        out_hbm,
        weight_ref,
        first_ref,
        second_ref,
        out_ref,
        woven_ref,
        sems,
    )
    adam_kernel(
        pair_ref,
        pick_ref,
        weight_ref,
        first_ref,
        second_ref,
        new_weight_hbm,
        new_first_hbm,
        new_second_hbm,
        made_ref,
        made_sems,
    )
    for copy in copies:
        copy.wait()


HBM = pl.BlockSpec(memory_space=pltpu.HBM)
VMEM = pl.BlockSpec(memory_space=pltpu.VMEM)


def call(kernel, outs, *arrays, scratch=(), far=(), far_out=(), near_out=False):
    arrays = [
        pltpu.with_memory_space_constraint(a, pltpu.HBM) if n in far else a
        for n, a in enumerate(arrays)
    ]
    place = pltpu.VMEM if near_out else jax.ShapeDtypeStruct
    return pl.pallas_call(
        kernel,
        out_shape=[place(shape, dtype) for shape, dtype in outs],
        in_specs=[HBM if n in far else VMEM for n in range(len(arrays))],
        out_specs=[HBM if n in far_out else VMEM for n in range(len(outs))],
        scratch_shapes=list(scratch),
        compiler_params=pltpu.CompilerParams(vmem_limit_bytes=24 * 1024 * 1024),
    )(*arrays)


def exchange(array, axis):
    groups = [GRID_ORDER if axis == "grid" else DP_ORDER]
    return lax.all_to_all(
        array, axis, split_axis=0, concat_axis=0, axis_index_groups=groups, tiled=True
    )


def shards(
    in_field, out_grad, point_weight, point_bias, spectral_weight, first_moment, second_moment
):
    forward, inverse, to_modes, to_rows, pick = (jnp.asarray(t) for t in tables())
    field = in_field.reshape(SLAB * C, NY)
    cotangent = out_grad.reshape(SLAB * C, NY)
    zero = jnp.zeros_like(point_weight)
    point = jnp.block([[point_weight, zero], [zero, point_weight]])
    bias = jnp.concatenate([point_bias, point_bias]).reshape(128, 1)
    message = [((512, 128), bf16)]

    plane = pltpu.VMEM((512, 512), bf16)
    woven = pltpu.VMEM((512, 128), f32)
    dma = pltpu.SemaphoreType.DMA

    (sent,) = call(
        spectra_kernel,
        message,
        field,
        forward,
        far=(0, 1),
        scratch=(plane, pltpu.VMEM((128, 512), bf16), woven, dma((2,))),
    )
    columns = exchange(sent, "grid")

    local = spectral_weight.astype(bf16).reshape(8, 2, C, C).transpose(0, 2, 1, 3).reshape(512, 128)
    (copies,) = call(copies_kernel, [((BLOCKS * 512, 128), bf16)], local, near_out=True)
    whole = exchange(copies, "dp")

    (modes,) = call(modes_kernel, [((128, 128), bf16)], columns, to_modes)
    linear, near = call(
        linear_kernel,
        [((512, 512), f32), ((512, 512), bf16)],
        field,
        cotangent,
        point.T,
        bias,
        far=(1,),
        scratch=(dma((1,)),),
        near_out=True,
    )
    modes, linear, near = lax.optimization_barrier((modes, linear, near))
    (sent,) = call(forward_modes_kernel, message, modes, whole, to_rows)
    received = exchange(sent, "grid")
    pre_grad, sent = call(
        slope_kernel,
        [((512, 512), bf16)] + message,
        received,
        linear,
        near,
        inverse,
        scratch=(woven,),
    )
    columns = exchange(sent, "grid")
    pair, sent = call(
        backward_modes_kernel,
        [((128, 128), bf16)] + message,
        columns,
        whole,
        modes,
        to_modes,
        to_rows,
    )
    received, pair = lax.optimization_barrier((exchange(sent, "grid"), pair))
    pair = exchange(pair, "dp")
    masters = [
        m.reshape(8, 2, C // 2, 128).transpose(0, 2, 1, 3).reshape(512, 128)
        for m in (spectral_weight, first_moment, second_moment)
    ]
    flat = [((512, 128), f32)] * 3
    held = pltpu.VMEM((512, 128), f32)
    grad_field, *made = call(
        last_kernel,
        [((512, 512), bf16)] + flat,
        received,
        pre_grad,
        point,
        forward,
        *masters,
        pair,
        pick,
        far=(4, 5, 6),
        far_out=(0, 1, 2, 3),
        scratch=(
            held,
            held,
            held,
            plane,
            woven,
            pltpu.VMEM((3, 512, 128), f32),
            dma((QUAD + 3,)),
            dma((12,)),
        ),
    )
    new_weight, new_first, new_second = (
        m.reshape(8, C // 2, 2, 128).transpose(0, 2, 1, 3).reshape(spectral_weight.shape)
        for m in made
    )
    return (grad_field.reshape(in_field.shape), new_weight, new_first, new_second)


def solution(mesh):
    split = P("dp", "grid", None, None)
    return jax.shard_map(
        shards,
        mesh=mesh,
        in_specs=(split, split, P(), P(), split, split, split),
        out_specs=(split, split, split, split),
        check_vma=False,
    )
```

```python
import math

import jax
import jax.numpy as jnp
import numpy as np
from jax import lax
from jax.experimental import pallas as pl
from jax.experimental.pallas import tpu as pltpu
from jax.sharding import PartitionSpec as P

C = 64
NX = 512
NY = 512
MX = 64
MY = 64
SLAB = 8
QUAD = 4
HALF = 64
BLOCKS = 8

GRID_ORDER = [(20 + 25 * k) % 64 for k in range(64)]
DP_ORDER = [(5 + 3 * k) % 8 for k in range(8)]

beta_one = 0.9
beta_two = 0.999
learn_rate = 0.01
adam_step = 100
epsilon_adam = 1e-08

f32 = jnp.float32
bf16 = jnp.bfloat16


def tables():
    frequency = np.array(GRID_ORDER)
    position = np.arange(NY)
    angles = ((position[:, None] * frequency[None, :]) % NY).astype(np.float32) * np.float32(
        2.0 * math.pi / NY
    )
    cos, sin = np.cos(angles), np.sin(angles)
    forward = np.stack([cos, -sin], axis=-1).reshape(NY, 2 * MY).T
    factor = np.where(frequency == 0, 1.0, 2.0).astype(np.float32) / np.float32(NX * NY)
    inverse = np.stack([factor * cos, -factor * sin], axis=-1).reshape(NY, 2 * MY).T

    column = np.arange(MX)
    wavenumber = np.where(column < MX // 2, column, NX - MX + column)
    rows = np.arange(NX)
    turn = ((wavenumber[:, None] * rows[None, :]) % NX).astype(np.float32) * np.float32(
        2.0 * math.pi / NX
    )
    by_order = lambda t: (
        t.reshape(BLOCKS, 8, NX // SLAB, SLAB)[DP_ORDER][:, :, GRID_ORDER].reshape(MX, NX)
    )
    col_cos, col_sin = by_order(np.cos(turn)), by_order(np.sin(turn))

    by_slab = lambda t: t.reshape(BLOCKS, 8, NX // SLAB, QUAD, 2)
    c, s = by_slab(col_cos), by_slab(col_sin)
    to_modes = np.stack([np.stack([c, s], 0), np.stack([-s, c], 0)], 0)
    to_modes = to_modes.transpose(6, 2, 0, 3, 4, 1, 5).reshape(256, 512)

    by_slab = lambda t: t.reshape(MX, NX // SLAB, QUAD, 2)
    c, s = by_slab(col_cos), by_slab(col_sin)
    to_rows = np.stack([np.stack([c, -s], 0), np.stack([s, c], 0)], 0)
    to_rows = to_rows.transpose(3, 0, 4, 1, 5, 2).reshape(512, 256)

    pick = np.zeros((2, 128, 2, C // 2, 2), np.float32)
    for c in range(C):
        for p in range(2):
            pick[p, c, c % 2, c // 2, p] = 1.0
    pick = pick.reshape(256, 128)
    made = (forward, inverse, to_modes, to_rows, pick)
    return tuple(np.asarray(t, np.float32).astype(jnp.bfloat16) for t in made)


def mm(a, b):
    return lax.dot_general(a, b, (((1,), (0,)), ((), ())), preferred_element_type=f32)


def mm_nt(a, b):
    return lax.dot_general(a, b, (((1,), (1,)), ((), ())), preferred_element_type=f32)


def mm_tn(a, b):
    return lax.dot_general(a, b, (((0,), (0,)), ((), ())), preferred_element_type=f32)


def low_lanes(shape):
    return lax.broadcasted_iota(jnp.int32, shape, len(shape) - 1) % 128 < HALF


def swap(value):
    return jnp.concatenate([value[:, HALF:], value[:, :HALF]], axis=1)


def part(q):
    return slice(q * 128, (q + 1) * 128)


def quarter(q):
    return pl.ds(q, 128, stride=QUAD)


def modes_of(received, to_modes):
    both = mm(to_modes, received)
    chosen = jnp.where(low_lanes((128, 128)), both[:128], both[128:])
    return (chosen + swap(chosen)).astype(bf16)


def rows_of(modes, to_rows):
    low = low_lanes((MX, 128))
    turned = swap(modes)
    stacked = jnp.concatenate(
        [
            jnp.where(low, modes, 0.0),
            jnp.where(low, 0.0, turned),
            jnp.where(low, turned, 0.0),
            jnp.where(low, 0.0, modes),
        ],
        axis=0,
    ).astype(bf16)
    return mm(to_rows, stacked).astype(bf16)


def own_block(shape):
    return (
        lax.broadcasted_iota(jnp.int32, shape, 0) % 8
        == lax.broadcasted_iota(jnp.int32, shape, 1) // HALF
    )


def gelu_slope(value):
    return 0.5 * (1.0 + lax.erf(value / math.sqrt(2.0))) + value * jnp.exp(
        -0.5 * value * value
    ) / math.sqrt(2.0 * math.pi)


def spectra_kernel(field_hbm, table_hbm, out_ref, field_ref, table_ref, woven_ref, sems):
    copies = [
        pltpu.make_async_copy(field_hbm, field_ref, sems.at[0]),
        pltpu.make_async_copy(table_hbm, table_ref, sems.at[1]),
    ]
    for copy in copies:
        copy.start()
    for copy in copies:
        copy.wait()
    table = table_ref[...]
    for q in range(QUAD):
        woven_ref[quarter(q), :] = mm_nt(table, field_ref[part(q), :])
    out_ref[...] = woven_ref[...].astype(bf16)


def copies_kernel(local_ref, out_ref):
    for block in range(BLOCKS):
        out_ref[block * 512 : (block + 1) * 512, :] = local_ref[...]


def modes_kernel(received_ref, to_modes_ref, modes_ref):
    modes_ref[...] = modes_of(received_ref[...], to_modes_ref[...])


def forward_modes_kernel(modes_ref, weight_ref, to_rows_ref, out_ref):
    wide = modes_ref[...].astype(f32)
    own = own_block((16, 512))
    sign = jnp.where(low_lanes((8, 128)), -1.0, 1.0)
    mixed = []
    for block in range(BLOCKS):
        mine = wide[block * 16 : (block + 1) * 16]
        spread = jnp.where(own, jnp.concatenate([mine] * 4, axis=1), 0.0).astype(bf16)
        product = mm(spread, weight_ref[block * 512 : (block + 1) * 512, :])
        mixed.append(product[:8] + sign * swap(product[8:]))
    out_ref[...] = rows_of(jnp.concatenate(mixed, axis=0), to_rows_ref[...])


def backward_modes_kernel(
    received_ref, weight_ref, modes_ref, to_modes_ref, to_rows_ref, pair_ref, out_ref
):
    grads = modes_of(received_ref[...], to_modes_ref[...])
    wide = grads.astype(f32)
    pair_ref[...] = jnp.where(
        low_lanes((128, 128)), modes_ref[...].astype(f32), wide
    ).astype(bf16)
    own = own_block((16, 512))
    low = low_lanes((8, 128))
    mixed = []
    for block in range(BLOCKS):
        real = wide[block * 16 : block * 16 + 8]
        imaginary = wide[block * 16 + 8 : block * 16 + 16]
        turned = jnp.concatenate(
            [jnp.where(low, real, imaginary), jnp.where(low, imaginary, -real)], axis=0
        ).astype(bf16)
        product = mm_nt(turned, weight_ref[block * 512 : (block + 1) * 512, :])
        product = jnp.where(own, product, 0.0)
        folded = product[:, :128] + product[:, 128:256] + product[:, 256:384] + product[:, 384:]
        folded = folded + swap(folded)
        mixed.append(jnp.where(low, folded[:8], folded[8:]))
    out_ref[...] = rows_of(jnp.concatenate(mixed, axis=0), to_rows_ref[...])


def linear_kernel(field_ref, cotangent_hbm, point_ref, bias_ref, out_ref, cotangent_ref, sems):
    copy = pltpu.make_async_copy(cotangent_hbm, cotangent_ref, sems.at[0])
    copy.start()
    for q in range(QUAD):
        out_ref[part(q), :] = mm(point_ref[...], field_ref[part(q), :]) + bias_ref[...]
    copy.wait()


def slope_kernel(
    received_ref, linear_ref, cotangent_ref, inverse_ref, grad_ref, out_ref, woven_ref
):
    inverse = inverse_ref[...]
    woven_ref[...] = received_ref[...].astype(f32)
    rows = [woven_ref[quarter(q), :].astype(bf16) for q in range(QUAD)]
    for q in range(QUAD):
        value = mm_tn(rows[q], inverse) + linear_ref[part(q), :]
        grad = (cotangent_ref[part(q), :].astype(f32) * gelu_slope(value)).astype(bf16)
        grad_ref[part(q), :] = grad
        woven_ref[quarter(q), :] = mm_nt(inverse, grad)
    out_ref[...] = woven_ref[...].astype(bf16)


def field_kernel(
    received_ref,
    grad_ref,
    point_ref,
    forward_ref,
    weight_hbm,
    first_hbm,
    second_hbm,
    out_hbm,
    weight_out,
    first_out,
    second_out,
    out_ref,
    woven_ref,
    sems,
):
    loads = []
    for n, (source, target) in enumerate(
        ((weight_hbm, weight_out), (first_hbm, first_out), (second_hbm, second_out))
    ):
        copy = pltpu.make_async_copy(source, target, sems.at[QUAD + n])
        copy.start()
        loads.append(copy)
    forward = forward_ref[...]
    woven_ref[...] = received_ref[...].astype(f32)
    copies = []
    for q in range(QUAD):
        rows = woven_ref[quarter(q), :].astype(bf16)
        value = mm_tn(rows, forward) + mm(point_ref[...], grad_ref[part(q), :])
        out_ref[part(q), :] = value.astype(bf16)
        copy = pltpu.make_async_copy(out_ref.at[part(q)], out_hbm.at[part(q)], sems.at[q])
        copy.start()
        copies.append(copy)
    for copy in loads + copies:
        copy.wait()


def adam_kernel(
    pair_ref,
    pick_ref,
    weight_ref,
    first_ref,
    second_ref,
    new_weight_hbm,
    new_first_hbm,
    new_second_hbm,
    made_ref,
    sems,
):
    bias_one = 1.0 - beta_one**adam_step
    bias_two = 1.0 - beta_two**adam_step
    wide = pair_ref[...].astype(f32)
    turned = []
    for sample in range(8):
        turned.append(-wide[sample * 16 + 8 : sample * 16 + 16])
        turned.append(wide[sample * 16 : sample * 16 + 8])
    both = jnp.concatenate([wide, jnp.concatenate(turned, axis=0)], axis=1).astype(bf16)
    left = mm(both, pick_ref[...])
    left = jnp.concatenate([left, swap(left)], axis=0).astype(bf16)
    low = low_lanes((128, 128))
    right = jnp.concatenate([jnp.where(low, swap(wide), 0.0), jnp.where(low, 0.0, wide)], axis=0)
    mode = lax.broadcasted_iota(jnp.int32, (256, 128), 0) % 8
    spread = [jnp.where(mode == j, right, 0.0).astype(bf16) for j in range(8)]
    gradients = mm_tn(left, jnp.concatenate(spread, axis=1))
    copies = []
    for j in range(8):
        at = slice(j * 64, (j + 1) * 64)
        gradient = gradients[:64, j * 128 : (j + 1) * 128]
        first = beta_one * first_ref[at, :] + (1.0 - beta_one) * gradient
        second = beta_two * second_ref[at, :] + (1.0 - beta_two) * gradient * gradient
        step = learn_rate * (first / bias_one) / (jnp.sqrt(second / bias_two) + epsilon_adam)
        made_ref[0, at, :] = weight_ref[at, :] - step
        made_ref[1, at, :] = first
        made_ref[2, at, :] = second
        if j % 2 == 1:
            at = slice((j - 1) * 64, (j + 1) * 64)
            for n, target in enumerate((new_weight_hbm, new_first_hbm, new_second_hbm)):
                copy = pltpu.make_async_copy(
                    made_ref.at[n, at], target.at[at], sems.at[3 * (j // 2) + n]
                )
                copy.start()
                copies.append(copy)
    for copy in copies:
        copy.wait()


HBM = pl.BlockSpec(memory_space=pltpu.HBM)
VMEM = pl.BlockSpec(memory_space=pltpu.VMEM)


def call(kernel, outs, *arrays, scratch=(), far=(), far_out=(), near_out=False):
    arrays = [
        pltpu.with_memory_space_constraint(a, pltpu.HBM) if n in far else a
        for n, a in enumerate(arrays)
    ]
    place = pltpu.VMEM if near_out else jax.ShapeDtypeStruct
    return pl.pallas_call(
        kernel,
        out_shape=[place(shape, dtype) for shape, dtype in outs],
        in_specs=[HBM if n in far else VMEM for n in range(len(arrays))],
        out_specs=[HBM if n in far_out else VMEM for n in range(len(outs))],
        scratch_shapes=list(scratch),
        compiler_params=pltpu.CompilerParams(vmem_limit_bytes=24 * 1024 * 1024),
    )(*arrays)


def exchange(array, axis):
    groups = [GRID_ORDER if axis == "grid" else DP_ORDER]
    return lax.all_to_all(
        array, axis, split_axis=0, concat_axis=0, axis_index_groups=groups, tiled=True
    )


def shards(
    in_field, out_grad, point_weight, point_bias, spectral_weight, first_moment, second_moment
):
    forward, inverse, to_modes, to_rows, pick = (jnp.asarray(t) for t in tables())
    field = in_field.reshape(SLAB * C, NY)
    cotangent = out_grad.reshape(SLAB * C, NY)
    zero = jnp.zeros_like(point_weight)
    point = jnp.block([[point_weight, zero], [zero, point_weight]])
    bias = jnp.concatenate([point_bias, point_bias]).reshape(128, 1)
    message = [((512, 128), bf16)]

    plane = pltpu.VMEM((512, 512), bf16)
    woven = pltpu.VMEM((512, 128), f32)
    dma = pltpu.SemaphoreType.DMA

    (sent,) = call(
        spectra_kernel,
        message,
        field,
        forward,
        far=(0, 1),
        scratch=(plane, pltpu.VMEM((128, 512), bf16), woven, dma((2,))),
    )
    columns = exchange(sent, "grid")

    local = spectral_weight.astype(bf16).reshape(8, 2, C, C).transpose(0, 2, 1, 3).reshape(512, 128)
    (copies,) = call(copies_kernel, [((BLOCKS * 512, 128), bf16)], local, near_out=True)
    whole = exchange(copies, "dp")

    (modes,) = call(modes_kernel, [((128, 128), bf16)], columns, to_modes)
    linear, near = call(
        linear_kernel,
        [((512, 512), f32), ((512, 512), bf16)],
        field,
        cotangent,
        point.T,
        bias,
        far=(1,),
        scratch=(dma((1,)),),
        near_out=True,
    )
    modes, linear, near = lax.optimization_barrier((modes, linear, near))
    (sent,) = call(forward_modes_kernel, message, modes, whole, to_rows)
    received = exchange(sent, "grid")
    pre_grad, sent = call(
        slope_kernel,
        [((512, 512), bf16)] + message,
        received,
        linear,
        near,
        inverse,
        scratch=(woven,),
    )
    columns = exchange(sent, "grid")
    pair, sent = call(
        backward_modes_kernel,
        [((128, 128), bf16)] + message,
        columns,
        whole,
        modes,
        to_modes,
        to_rows,
    )
    received, pair = lax.optimization_barrier((exchange(sent, "grid"), pair))
    pair = exchange(pair, "dp")
    masters = [
        m.reshape(8, 2, C // 2, 128).transpose(0, 2, 1, 3).reshape(512, 128)
        for m in (spectral_weight, first_moment, second_moment)
    ]
    flat = [((512, 128), f32)] * 3
    grad_field, *near = call(
        field_kernel,
        [((512, 512), bf16)] + flat,
        received,
        pre_grad,
        point,
        forward,
        *masters,
        far=(4, 5, 6),
        far_out=(0,),
        scratch=(plane, woven, dma((QUAD + 3,))),
    )
    made = call(
        adam_kernel,
        flat,
        pair,
        pick,
        *near,
        far_out=(0, 1, 2),
        scratch=(pltpu.VMEM((3, 512, 128), f32), dma((12,))),
    )
    new_weight, new_first, new_second = (
        m.reshape(8, C // 2, 2, 128).transpose(0, 2, 1, 3).reshape(spectral_weight.shape)
        for m in made
    )
    return (grad_field.reshape(in_field.shape), new_weight, new_first, new_second)


def solution(mesh):
    split = P("dp", "grid", None, None)
    return jax.shard_map(
        shards,
        mesh=mesh,
        in_specs=(split, split, P(), P(), split, split, split),
        out_specs=(split, split, split, split),
        check_vma=False,
    )
```
